512 devices in a mesh: section: 8 (over x, core), expert: 8 (over z_lo), dp: 8 (over y, z_hi).
Axes of the slice: x: 4, y: 4, z: 16 (z_hi: 2, z_lo: 8; z = z_hi * 8 + z_lo), core: 2. Of those that a mesh axis runs over, the one named last changes fastest.
Arguments:
- layer_input: bfloat16 [8, 8192, 2048], P('section', ('expert', 'dp')), may hold values from -6 to 6
- output_grad: bfloat16 [8, 8192, 2048], P('section', ('expert', 'dp')), may hold values from -6 to 6
- expert_ids: int32 [8, 8192], P('section', ('expert', 'dp')), may hold values from 0 to 63, as said below
- w_gate: bfloat16 [8, 2048, 8192], P('section', None, ('expert', 'dp')), may hold values from -0.125 to 0.125
- w_up: bfloat16 [8, 2048, 8192], P('section', None, ('expert', 'dp')), may hold values from -0.125 to 0.125
- w_down: bfloat16 [8, 2048, 8192], P('section', None, ('expert', 'dp')), may hold values from -0.0625 to 0.0625
Outputs:
- input_grad: bfloat16 [8, 8192, 2048], P('section', ('expert', 'dp'))
- grad_gate: bfloat16 [8, 2048, 8192], P('section', None, ('expert', 'dp'))
- grad_up: bfloat16 [8, 2048, 8192], P('section', None, ('expert', 'dp'))
- grad_down: bfloat16 [8, 2048, 8192], P('section', None, ('expert', 'dp'))
The draws below stay inside these ranges and needn't reach their ends.
Inputs may be any that keep to these rules, and one draw needn't show every extreme that they name: `expert_ids`: expert 0 is the expert of these weights. Every device's 128 tokens name expert 0 between 1 and 8 times, and on every section some device names it exactly 8 times.
All inputs are finite; a program needn't handle non-finite values.
Results may differ from the reference program's by a relative error of at most 0.0065.
Values may be sent and summed in bfloat16 or wider, within the bound.
A program may use at most 64 MiB of HBM per device.

```python
import jax
import jax.numpy as jnp
from jax import lax

D = 2048
HID = 8192
ALL_EXPERTS = 64
TOK_DEV = 128
SLOT = 8
SECTIONS = 8
TOKENS = 8192
ROWS = 512


def draw_expert_ids(key, part):
    groups = SECTIONS * (TOKENS // TOK_DEV)
    per_section = TOKENS // TOK_DEV
    key_count, key_full, key_order, key_other = jax.random.split(key, 4)
    counts = jax.random.randint(key_count, (groups,), 1, SLOT + 1).astype(jnp.int32)
    fullest = jax.random.randint(key_full, (SECTIONS,), 0, per_section).astype(jnp.int32)
    block_ids = jnp.arange(groups, dtype=jnp.int32)
    section_of = block_ids // per_section
    within_section = block_ids - section_of * per_section
    is_full = within_section == jnp.take(fullest, section_of)
    counts = jnp.where(is_full, SLOT, counts).astype(jnp.int32)
    scores = jax.random.randint(key_order, (groups, TOK_DEV), 0, 1 << 20).astype(jnp.int32)
    scores = scores * TOK_DEV + jnp.arange(TOK_DEV, dtype=jnp.int32)[None, :]
    ranks = jnp.argsort(jnp.argsort(scores, axis=1, stable=True), axis=1, stable=True).astype(jnp.int32)
    chosen = ranks < counts[:, None]
    others = jax.random.randint(key_other, (groups, TOK_DEV), 1, ALL_EXPERTS).astype(jnp.int32)
    labels = jnp.where(chosen, 0, others).astype(jnp.int32)
    return labels.reshape(SECTIONS, TOKENS)


def levels(own_key, shape, pieces, smallest, top_value):
    level, own = 1.0, jax.random.fold_in(own_key, 6)
    for position, blocks in pieces:
        steps = jnp.exp(jax.random.uniform(jax.random.fold_in(own, position), (blocks,), jnp.float32, smallest / len(pieces), top_value / len(pieces)))
        level = level * jnp.repeat(steps, shape[position] // blocks).reshape([-1 if axis == position else 1 for axis in range(len(shape))])
    return level


def noise(rng, dims, spread, limit, shards=(), held_as=jnp.bfloat16):
    drawn = jax.random.normal(rng, dims, jnp.float32) * spread
    if len(shards) > 0:
        drawn = levels(rng, dims, shards, -0.22, 0.18) * drawn
    return jnp.clip(drawn, min=-limit, max=limit).astype(held_as)


def setup_inputs(seed: int = 0) -> dict:
    splits = jax.random.split(jax.random.key(seed), 7)
    layer_input = noise(splits[0], (SECTIONS, TOKENS, D), 1.0, 6.0, ((0, 8), (1, 64)))
    output_grad = noise(splits[1], (SECTIONS, TOKENS, D), 1.0, 6.0, ((0, 8), (1, 64)))
    expert_ids = draw_expert_ids(jax.random.fold_in(splits[6], 71), 0)
    w_gate = noise(splits[3], (SECTIONS, D, HID), D ** -0.5, 0.125, ((0, 8), (2, 64)))
    w_up = noise(splits[4], (SECTIONS, D, HID), D ** -0.5, 0.125, ((0, 8), (2, 64)))
    w_down = noise(splits[5], (SECTIONS, D, HID), HID ** -0.5, 0.0625, ((0, 8), (2, 64)))
    return dict(layer_input=layer_input, output_grad=output_grad, expert_ids=expert_ids, w_gate=w_gate, w_up=w_up, w_down=w_down)


def slot_match(labels):
    chosen = (labels == 0).astype(jnp.int32)
    within = jnp.cumsum(chosen, axis=1) - chosen
    target = jnp.where(chosen > 0, within, SLOT).astype(jnp.int32)
    places = jnp.arange(SLOT, dtype=jnp.int32)
    return (target[:, None, :] == places[None, :, None]).astype(jnp.float32)


def expert_backward(x_rows, dy_rows, w_gate, w_up, w_down):
    gate = jnp.dot(x_rows, w_gate, preferred_element_type=jnp.float32)
    upper = jnp.dot(x_rows, w_up, preferred_element_type=jnp.float32)
    sigma = jax.nn.sigmoid(gate)
    active = gate * sigma
    hidden = (active * upper).astype(jnp.bfloat16)
    d_hidden = jnp.dot(dy_rows, w_down, preferred_element_type=jnp.float32)
    d_gate = (d_hidden * upper * sigma * (1.0 + gate * (1.0 - sigma))).astype(jnp.bfloat16)
    d_up = (d_hidden * active).astype(jnp.bfloat16)
    back_dims = (((1,), (1,)), ((), ()))
    d_input = lax.dot_general(d_gate, w_gate, back_dims, preferred_element_type=jnp.float32)
    d_input = d_input + lax.dot_general(d_up, w_up, back_dims, preferred_element_type=jnp.float32)
    row_dims = (((0,), (0,)), ((), ()))
    part_gate = lax.dot_general(x_rows, d_gate, row_dims, preferred_element_type=jnp.float32)
    part_up = lax.dot_general(x_rows, d_up, row_dims, preferred_element_type=jnp.float32)
    part_down = lax.dot_general(dy_rows, hidden, row_dims, preferred_element_type=jnp.float32)
    return d_input, part_gate, part_up, part_down


def section_reference(inputs, grads, routes, w_gate, w_up, w_down):
    groups = TOKENS // TOK_DEV
    match = slot_match(routes.reshape(groups, TOK_DEV))
    inputs_f = inputs.reshape(groups, TOK_DEV, D).astype(jnp.float32)
    grads_f = grads.reshape(groups, TOK_DEV, D).astype(jnp.float32)
    x_rows = jnp.einsum("gst,gtd->gsd", match, inputs_f).astype(jnp.bfloat16).reshape(ROWS, D)
    dy_rows = jnp.einsum("gst,gtd->gsd", match, grads_f).astype(jnp.bfloat16).reshape(ROWS, D)
    d_input, part_gate, part_up, part_down = expert_backward(x_rows, dy_rows, w_gate, w_up, w_down)
    d_rows = lax.optimization_barrier(d_input.astype(jnp.bfloat16))
    d_rows = d_rows.astype(jnp.float32).reshape(groups, SLOT, D)
    term = jnp.einsum("gst,gsd->gtd", match, d_rows)
    token_grad = (grads_f + term).astype(jnp.bfloat16).reshape(TOKENS, D)
    return (token_grad, part_gate.astype(jnp.bfloat16), part_up.astype(jnp.bfloat16),
            part_down.astype(jnp.bfloat16))


def reference(layer_input, output_grad, expert_ids, w_gate, w_up, w_down):
    def per_section(items):
        return section_reference(*items)

    token_grad, grad_gate, grad_up, grad_down = lax.map(
        per_section, (layer_input, output_grad, expert_ids, w_gate, w_up, w_down))
    input_grad = jnp.roll(token_grad, -1, axis=0)
    return input_grad, grad_gate, grad_up, grad_down
```

```python
import jax
import jax.numpy as jnp
from jax import lax
from jax.sharding import PartitionSpec as P

SLOT = 8


def shifted(value, axis, steps):
    count = lax.axis_size(axis)
    pairs = [(source, (source + steps) % count) for source in range(count)]
    return lax.ppermute(value, axis, pairs)


def unit_grads(x_rows, dy_rows, w_gate, w_up, w_down):
    gate = jnp.dot(x_rows, w_gate, preferred_element_type=jnp.float32)
    upper = jnp.dot(x_rows, w_up, preferred_element_type=jnp.float32)
    sigma = jax.nn.sigmoid(gate)
    active = gate * sigma
    hidden = (active * upper).astype(jnp.bfloat16)
    d_hidden = jnp.dot(dy_rows, w_down, preferred_element_type=jnp.float32)
    d_gate = (d_hidden * upper * sigma * (1.0 + gate * (1.0 - sigma))).astype(jnp.bfloat16)
    d_up = (d_hidden * active).astype(jnp.bfloat16)
    back_dims = (((1,), (1,)), ((), ()))
    d_input = lax.dot_general(d_gate, w_gate, back_dims, preferred_element_type=jnp.float32)
    d_input = d_input + lax.dot_general(d_up, w_up, back_dims, preferred_element_type=jnp.float32)
    return (d_input, d_gate, d_up, hidden)


def weight_grads(x_rows, dy_rows, d_gate, d_up, hidden):
    row_dims = (((0,), (0,)), ((), ()))
    part_gate = lax.dot_general(x_rows, d_gate, row_dims, preferred_element_type=jnp.float32)
    part_up = lax.dot_general(x_rows, d_up, row_dims, preferred_element_type=jnp.float32)
    part_down = lax.dot_general(dy_rows, hidden, row_dims, preferred_element_type=jnp.float32)
    return (part_gate, part_up, part_down)


def body(layer_input, output_grad, expert_ids, w_gate, w_up, w_down):
    inputs = layer_input[0]
    grads = output_grad[0]
    routes = expert_ids[0]
    chosen = (routes == 0).astype(jnp.int32)
    order = jnp.arange(chosen.shape[0], dtype=jnp.int32)
    within = jnp.sum(jnp.where(order[None, :] < order[:, None], chosen[None, :], 0), axis=1)
    target = jnp.where(chosen > 0, within, SLOT)
    places = jnp.arange(SLOT, dtype=jnp.int32)
    match = (target[None, :] == places[:, None]).astype(jnp.bfloat16)
    send_x = jnp.dot(match, inputs, preferred_element_type=jnp.float32).astype(jnp.bfloat16)
    send_dy = jnp.dot(match, grads, preferred_element_type=jnp.float32).astype(jnp.bfloat16)
    group_x, group_dy = (
        lax.all_gather(send_x, "expert", axis=0, tiled=True),
        lax.all_gather(send_dy, "expert", axis=0, tiled=True),
    )
    full_gate, full_up, full_down = (
        lax.all_gather(w_gate[0], "dp", axis=1, tiled=True),
        lax.all_gather(w_up[0], "dp", axis=1, tiled=True),
        lax.all_gather(w_down[0], "dp", axis=1, tiled=True),
    )
    d_part, d_gate, d_up, hidden = unit_grads(group_x, group_dy, full_gate, full_up, full_down)
    mine = lax.psum_scatter(d_part.astype(jnp.bfloat16), "expert", scatter_dimension=0, tiled=True)
    own_gate, own_up, own_hidden = (
        lax.all_to_all(d_gate, "dp", split_axis=1, concat_axis=0, tiled=True),
        lax.all_to_all(d_up, "dp", split_axis=1, concat_axis=0, tiled=True),
        lax.all_to_all(hidden, "dp", split_axis=1, concat_axis=0, tiled=True),
    )
    every_x, every_dy = (
        lax.all_gather(group_x, "dp", axis=0, tiled=True),
        lax.all_gather(group_dy, "dp", axis=0, tiled=True),
    )
    part_gate, part_up, part_down = weight_grads(every_x, every_dy, own_gate, own_up, own_hidden)
    d_rows = lax.optimization_barrier(mine)
    term = lax.dot_general(
        match, d_rows, (((0,), (0,)), ((), ())), preferred_element_type=jnp.float32
    )
    token_grad = (grads.astype(jnp.float32) + term).astype(jnp.bfloat16)
    moved = shifted(token_grad, "section", -1)
    return (
        moved[None],
        part_gate.astype(jnp.bfloat16)[None],
        part_up.astype(jnp.bfloat16)[None],
        part_down.astype(jnp.bfloat16)[None],
    )


def solution(mesh):
    in_specs = (
        P("section", ("expert", "dp"), None),
        P("section", ("expert", "dp"), None),
        P("section", ("expert", "dp")),
        P("section", None, ("expert", "dp")),
        P("section", None, ("expert", "dp")),
        P("section", None, ("expert", "dp")),
    )
    out_specs = (
        P("section", ("expert", "dp"), None),
        P("section", None, ("expert", "dp")),
        P("section", None, ("expert", "dp")),
        P("section", None, ("expert", "dp")),
    )
    return jax.shard_map(body, mesh=mesh, in_specs=in_specs, out_specs=out_specs, check_vma=False)
```

```python
import jax
import jax.numpy as jnp
from jax import lax
from jax.sharding import PartitionSpec as P

SLOT = 8
GROUP = ("expert", "dp")


def shifted(value, axis, steps):
    count = lax.axis_size(axis)
    pairs = [(source, (source + steps) % count) for source in range(count)]
    return lax.ppermute(value, axis, pairs)


def body(layer_input, output_grad, expert_ids, w_gate, w_up, w_down):
    inputs = layer_input[0]
    grads = output_grad[0]
    routes = expert_ids[0]
    chosen = (routes == 0).astype(jnp.int32)
    order = jnp.arange(chosen.shape[0], dtype=jnp.int32)
    within = jnp.sum(jnp.where(order[None, :] < order[:, None], chosen[None, :], 0), axis=1)
    target = jnp.where(chosen > 0, within, SLOT)
    places = jnp.arange(SLOT, dtype=jnp.int32)
    match = (target[None, :] == places[:, None]).astype(jnp.bfloat16)
    send_x = jnp.dot(match, inputs, preferred_element_type=jnp.float32).astype(jnp.bfloat16)
    send_dy = jnp.dot(match, grads, preferred_element_type=jnp.float32).astype(jnp.bfloat16)
    moved_grads = shifted(grads, "section", -1)
    moved_match = shifted(match, "section", -1)
    rows = lax.all_gather(jnp.stack([send_x, send_dy]), GROUP, axis=1, tiled=True)
    x_rows, dy_rows = rows[0], rows[1]
    w_both = jnp.concatenate([w_gate[0], w_up[0]], axis=1)
    both = jnp.dot(x_rows, w_both, preferred_element_type=jnp.float32)
    width = w_gate.shape[2]
    gate, upper = both[:, :width], both[:, width:]
    sigma = jax.nn.sigmoid(gate)
    active = gate * sigma
    hidden = (active * upper).astype(jnp.bfloat16)
    d_hidden = jnp.dot(dy_rows, w_down[0], preferred_element_type=jnp.float32)
    d_gate = (d_hidden * upper * sigma * (1.0 + gate * (1.0 - sigma))).astype(jnp.bfloat16)
    d_up = (d_hidden * active).astype(jnp.bfloat16)
    d_both = jnp.concatenate([d_gate, d_up], axis=1)
    back_dims = (((1,), (1,)), ((), ()))
    d_part = lax.dot_general(d_both, w_both, back_dims, preferred_element_type=jnp.float32)
    d_rows = lax.psum_scatter(d_part.astype(jnp.bfloat16), GROUP, scatter_dimension=0, tiled=True)
    d_rows = shifted(d_rows, "section", -1)
    row_dims = (((0,), (0,)), ((), ()))
    part_both = lax.dot_general(x_rows, d_both, row_dims, preferred_element_type=jnp.float32).astype(jnp.bfloat16)
    part_down = lax.dot_general(dy_rows, hidden, row_dims, preferred_element_type=jnp.float32).astype(jnp.bfloat16)
    term = lax.dot_general(
        moved_match, d_rows, (((0,), (0,)), ((), ())), preferred_element_type=jnp.float32
    )
    token_grad = (moved_grads.astype(jnp.float32) + term).astype(jnp.bfloat16)
    return (token_grad[None], part_both[None, :, :width], part_both[None, :, width:], part_down[None])


def solution(mesh):
    rows = P("section", ("expert", "dp"), None)
    weights = P("section", None, ("expert", "dp"))
    in_specs = (rows, rows, P("section", ("expert", "dp")), weights, weights, weights)
    out_specs = (rows, weights, weights, weights)
    return jax.shard_map(body, mesh=mesh, in_specs=in_specs, out_specs=out_specs, check_vma=False)
```

```python
import functools

import jax
import jax.numpy as jnp
from jax import lax
from jax.experimental import pallas as pl
from jax.experimental.pallas import tpu as pltpu
from jax.sharding import PartitionSpec as P

SLOT = 8
Z_HI = 2
F32 = jnp.float32
BF16 = jnp.bfloat16
ROWS_DIM = (((0,), (0,)), ((), ()))
BACK_DIM = (((1,), (1,)), ((), ()))


def slot_match(ids):
    tokens = ids.shape[1]
    chosen = jnp.broadcast_to((ids == 0).astype(F32), (SLOT, tokens))
    before = lax.broadcasted_iota(jnp.int32, (tokens, tokens), 0)
    after = lax.broadcasted_iota(jnp.int32, (tokens, tokens), 1)
    order = (before < after).astype(F32).astype(BF16)
    within = jnp.dot(chosen.astype(BF16), order, preferred_element_type=F32)
    place = lax.broadcasted_iota(jnp.int32, (SLOT, tokens), 0).astype(F32)
    return jnp.where(within == place, chosen, 0.0).astype(BF16)


def kernel(cfg, ids_ref, x_ref, dy_ref, wg_ref, wu_ref, wd_ref, og_ref, gg_ref, gu_ref, gd_ref,
           x_v, dy_v, w_gu, w_dn, shift_dy, shift_ids, g_a, g_b, x_all, dy_all, d_gu, hid, p_a, p_b,
           sa_r, ra_r, sa_l, ra_l, sy_b, ry_b, sum_b, sb_r, rb_r, sb_l, rb_l, sy_a, ry_a, fin_a, fin_b, got_a, got_b,
           og_v, gg_v, gu_v, gd_v,
           loc, sh_s, sh_r, a1_s, a1_r, ar_s, ar_r, al_s, al_r, br_s, br_r, bl_s, bl_r, by_s, by_r,
           rar_s, rar_r, ral_s, ral_r, rby_s, rby_r, rbr_s, rbr_r, rbl_s, rbl_r, ray_s, ray_r):
    Y, Z, D, CA, RA = cfg
    HA, HB = RA // 2, (D - RA) // 2
    K = Z // 2
    n_sec, n_exp = lax.axis_size("section"), lax.axis_size("expert")
    sec, ex, dp = lax.axis_index("section"), lax.axis_index("expert"), lax.axis_index("dp")
    y, z = dp // Z_HI, lax.rem(dp, Z_HI) * n_exp + ex

    def wrap(v, n):
        return lax.rem(v + n, n)

    def at(yy, zz):
        return {"expert": lax.rem(zz, n_exp), "dp": yy * Z_HI + zz // n_exp}

    z_right, z_left = at(y, wrap(z + 1, Z)), at(y, wrap(z - 1, Z))
    y_right, y_left = at(wrap(y + 1, Y), z), at(wrap(y - 1, Y), z)
    y_far = at(wrap(y + 2, Y), z)
    s_prev, s_next = {"section": wrap(sec - 1, n_sec)}, {"section": wrap(sec + 1, n_sec)}

    def remote(src, dst, s_sem, r_sem, to):
        return pltpu.make_async_remote_copy(
            src_ref=src, dst_ref=dst, send_sem=s_sem, recv_sem=r_sem, device_id=to, device_id_type=pl.DeviceIdType.MESH)

    barrier = pltpu.get_barrier_semaphore()
    partners = (z_right, z_left, y_right, y_left, y_far, s_prev, s_next)
    for to in partners:
        pl.semaphore_signal(barrier, inc=1, device_id=to, device_id_type=pl.DeviceIdType.MESH)

    half = w_gu.shape[1] // 2
    loads = [
        pltpu.make_async_copy(x_ref, x_v, loc.at[0]),
        pltpu.make_async_copy(dy_ref, dy_v, loc.at[1]),
        pltpu.make_async_copy(wg_ref, w_gu.at[:, pl.ds(0, half)], loc.at[2]),
        pltpu.make_async_copy(wu_ref, w_gu.at[:, pl.ds(half, half)], loc.at[3]),
        pltpu.make_async_copy(wd_ref, w_dn, loc.at[4]),
    ]
    for copy in loads:
        copy.start()
    match = slot_match(ids_ref[...])
    loads[0].wait()
    loads[1].wait()
    own = jnp.concatenate([
        jnp.dot(match, x_v[...], preferred_element_type=F32),
        jnp.dot(match, dy_v[...], preferred_element_type=F32)], axis=0).astype(BF16)
    g_a[z, y] = own[:, :CA]
    g_b[z, y] = own[:, CA:]
    pl.semaphore_wait(barrier, len(partners))

    def a1(j, to):
        return remote(g_a.at[z, y], g_a.at[z, y], a1_s.at[j], a1_r.at[j], to)

    def a1_in(j, yy):
        return remote(g_a.at[z, yy], g_a.at[z, yy], a1_s.at[j], a1_r.at[j], y_right)

    def a_right(k, block):
        return remote(g_a.at[block], g_a.at[block], ar_s.at[k], ar_r.at[k], z_right)

    def a_left(k, block):
        return remote(g_a.at[block], g_a.at[block], al_s.at[k], al_r.at[k], z_left)

    def b_right(k, block):
        return remote(g_b.at[block, y], g_b.at[block, y], br_s.at[k], br_r.at[k], z_right)

    def b_left(k, block):
        return remote(g_b.at[block, y], g_b.at[block, y], bl_s.at[k], bl_r.at[k], z_left)

    def b_y(kind, o, yy, to):
        block = wrap(z - o, Z)
        return remote(g_b.at[block, yy], g_b.at[block, yy], by_s.at[kind, o], by_r.at[kind, o], to)

    def spread(o):
        b_y(0, o, y, y_right).start()
        b_y(1, o, y, y_left).start()

    for j, to in enumerate((y_right, y_left, y_far)):
        a1(j, to).start()
    b_right(0, z).start()
    b_left(0, z).start()
    spread(0)
    shift = [remote(ids_ref, shift_ids, sh_s.at[0], sh_r.at[0], s_prev), remote(dy_ref, shift_dy, sh_s.at[1], sh_r.at[1], s_prev)]
    for copy in shift:
        copy.start()
    for j, step in enumerate((-1, 1, 2)):
        a1_in(j, wrap(y + step, Y)).wait_recv()
    a_right(0, z).start()
    a_left(0, z).start()

    def pass_right(o):
        b_y(0, o, wrap(y - 1, Y), y_right).wait_recv()
        b_y(2, o, wrap(y - 1, Y), y_right).start()

    def pass_left(o):
        b_y(1, o, wrap(y + 1, Y), y_left).wait_recv()
        b_y(2, o, wrap(y + 1, Y), y_left).start()

    def gather_step(k, _):
        zr, zl = wrap(z - k, Z), wrap(z + k, Z)

        @pl.when(k < K)
        def _():
            b_right(k - 1, zr).wait_recv()

            @pl.when(k < K - 1)
            def _():
                b_right(k, zr).start()

            spread(k)

        b_left(k - 1, zl).wait_recv()

        @pl.when(k < K)
        def _():
            b_left(k, zl).start()

        spread(Z - k)
        a_right(k - 1, zr).wait_recv()

        @pl.when(k < K)
        def _():
            a_right(k, zr).start()
            a_left(k - 1, zl).wait_recv()

            @pl.when(k < K - 1)
            def _():
                a_left(k, zl).start()

        pass_right(k - 1)

        @pl.when(k > 1)
        def _():
            pass_left(Z - k + 1)

        return 0

    lax.fori_loop(1, K + 1, gather_step, 0)
    pass_left(K)

    def gather_end(o, _):
        @pl.when(o < K)
        def _():
            b_y(1, o, wrap(y + 1, Y), y_left).wait_recv()

        @pl.when(o >= K)
        def _():
            b_y(0, o, wrap(y - 1, Y), y_right).wait_recv()

        b_y(2, o, wrap(y + 2, Y), y_right).wait_recv()
        return 0

    lax.fori_loop(0, Z, gather_end, 0)
    for copy in loads[2:]:
        copy.wait()

    CZ = 128 // (Y * SLOT)

    def unpack(c, _):
        rows = pl.ds(pl.multiple_of(c * (Y * SLOT), Y * SLOT), Y * SLOT)
        for ref, lo, hi in ((g_a, 0, CA), (g_b, CA, D)):
            both = ref[c].astype(F32)
            x_all[rows, lo:hi] = both[:, :SLOT].reshape(Y * SLOT, hi - lo).astype(BF16)
            dy_all[rows, lo:hi] = both[:, SLOT:].reshape(Y * SLOT, hi - lo).astype(BF16)
        return 0

    lax.fori_loop(0, Z, unpack, 0)

    def forward(c, _):
        rows = pl.ds(pl.multiple_of(c * 128, 128), 128)
        both = jnp.dot(x_all[rows, :], w_gu[...], preferred_element_type=F32)
        d_hidden = jnp.dot(dy_all[rows, :], w_dn[...], preferred_element_type=F32)
        gate, upper = both[:, :half], both[:, half:]
        sigma = jax.nn.sigmoid(gate)
        active = gate * sigma
        hid[rows, :] = (active * upper).astype(BF16)
        d_gu[rows, :half] = (d_hidden * upper * sigma * (1.0 + gate * (1.0 - sigma))).astype(BF16)
        d_gu[rows, half:] = (d_hidden * active).astype(BF16)
        CW = 256
        for lo in range(0, D, CW):
            part = lax.dot_general(d_gu[rows, :], w_gu[lo:lo + CW, :], BACK_DIM, preferred_element_type=F32)
            if lo < RA:
                p_a[pl.ds(c * CZ, CZ), :, lo:lo + CW] = part.reshape(CZ, Y * SLOT, CW)
            else:
                cut = part.reshape(CZ, Y, SLOT, CW)
                for yy in range(Y):
                    p_b[yy, pl.ds(c * CZ, CZ), :, lo - RA:lo - RA + CW] = cut[:, yy]
        return 0

    lax.fori_loop(0, Z // CZ, forward, 0)

    def ra_right(k):
        return remote(sa_r.at[k], ra_r.at[k], rar_s.at[k], rar_r.at[k], z_right)

    def ra_left(k):
        return remote(sa_l.at[k], ra_l.at[k], ral_s.at[k], ral_r.at[k], z_left)

    def rb_right(k):
        return remote(sb_r.at[k], rb_r.at[k], rbr_s.at[k], rbr_r.at[k], z_right)

    def rb_left(k):
        return remote(sb_l.at[k], rb_l.at[k], rbl_s.at[k], rbl_r.at[k], z_left)

    def rb_y(j):
        return remote(sy_b.at[j], ry_b.at[j], rby_s.at[j], rby_r.at[j], y_right if j % 2 == 0 else y_left)

    def ra_y(j, to):
        return remote(sy_a.at[j], ry_a.at[j], ray_s.at[j], ray_r.at[j], to)

    def ring_a(k):
        if k < K:
            value = p_a[wrap(z + K - k, Z)]
            if k > 0:
                ra_right(k - 1).wait_recv()
                value = value + ra_r[k - 1].astype(F32)
            sa_r[k] = value.astype(BF16)
            ra_right(k).start()
        if k < K - 1:
            value = p_a[wrap(z - K + 1 + k, Z)]
            if k > 0:
                ra_left(k - 1).wait_recv()
                value = value + ra_l[k - 1].astype(F32)
            sa_l[k] = value.astype(BF16)
            ra_left(k).start()

    def ring_b(k):
        if k < K - 1:
            value = sum_b[wrap(z + K - 1 - k, Z)]
            if k > 0:
                rb_right(k - 1).wait_recv()
                value = value + rb_r[k - 1].astype(F32)
            sb_r[k] = value.astype(BF16)
            rb_right(k).start()
        if k < K:
            value = sum_b[wrap(z - K + k, Z)]
            if k > 0:
                rb_left(k - 1).wait_recv()
                value = value + rb_l[k - 1].astype(F32)
            sb_l[k] = value.astype(BF16)
            rb_left(k).start()

    def flat(yy, lo):
        return p_b[yy, :, :, lo:lo + HB].reshape(Z * SLOT, HB)

    def y_first():
        far, nxt, prv = wrap(y + 2, Y), wrap(y + 1, Y), wrap(y - 1, Y)
        for j, value in enumerate((flat(far, 0), flat(far, HB), flat(nxt, HB), flat(prv, 0))):
            sy_b[j] = value.astype(BF16)
            rb_y(j).start()

    def y_second():
        nxt, prv = wrap(y + 1, Y), wrap(y - 1, Y)
        rb_y(0).wait_recv()
        sy_b[4] = (flat(nxt, 0) + ry_b[0].astype(F32)).astype(BF16)
        rb_y(4).start()
        rb_y(1).wait_recv()
        sy_b[5] = (flat(prv, HB) + ry_b[1].astype(F32)).astype(BF16)
        rb_y(5).start()

    def y_sum():
        for j in range(2, 6):
            rb_y(j).wait_recv()
        first = flat(y, 0) + ry_b[4].astype(F32) + ry_b[3].astype(F32)
        second = flat(y, HB) + ry_b[2].astype(F32) + ry_b[5].astype(F32)
        sum_b[:, :SLOT, :] = first.reshape(Z, SLOT, HB)
        sum_b[:, SLOT:, :] = second.reshape(Z, SLOT, HB)

    steps = 8
    WD = D // steps

    def weights(j):
        cols = slice(j * WD, (j + 1) * WD)
        part = lax.dot_general(x_all[:, cols], d_gu[...], ROWS_DIM, preferred_element_type=F32).astype(BF16)
        gg_v[cols, :] = part[:, :half]
        gu_v[cols, :] = part[:, half:]
        gd_v[cols, :] = lax.dot_general(dy_all[:, cols], hid[...], ROWS_DIM, preferred_element_type=F32).astype(BF16)

    todo = list(range(steps))

    def some_weights():
        if todo:
            weights(todo.pop(0))

    ring_a(0)
    y_first()
    some_weights()
    ring_a(1)
    y_second()
    some_weights()
    ring_a(2)
    some_weights()
    ring_a(3) if K > 3 else None
    y_sum()
    ring_b(0)
    some_weights()
    done_a, done_b = min(4, K), 1
    while done_a < K:
        ring_a(done_a)
        ring_b(done_b)
        done_a, done_b = done_a + 1, done_b + 1
        some_weights()
    while todo:
        some_weights()
    outs = [
        pltpu.make_async_copy(gg_v, gg_ref, loc.at[0]),
        pltpu.make_async_copy(gu_v, gu_ref, loc.at[1]),
        pltpu.make_async_copy(gd_v, gd_ref, loc.at[2]),
    ]
    for copy in outs:
        copy.start()
    ra_right(K - 1).wait_recv()
    ra_left(K - 2).wait_recv()
    total = p_a[z] + ra_r[K - 1].astype(F32) + ra_l[K - 2].astype(F32)
    total = total.reshape(Y, SLOT, RA)
    p_y = jnp.concatenate([total[:, :, :HA], total[:, :, HA:]], axis=1)
    fin_y = p_y.astype(BF16)
    for yy in range(Y):
        sy_a[3 + yy] = fin_y[yy]
    y_peers = ((wrap(y + 1, Y), y_right), (wrap(y - 1, Y), y_left), (wrap(y + 2, Y), y_far))
    for j, (yy, to) in enumerate(y_peers):
        sy_a[j] = sy_a[3 + yy]
        ra_y(j, to).start()
    while done_b < K:
        ring_b(done_b)
        done_b += 1
    for j in range(3):
        ra_y(j, y_right).wait_recv()
    value = sy_a[3 + y].astype(F32)
    for j in range(3):
        value = value + ry_a[j].astype(F32)
    fin_a[...] = value.astype(BF16)
    back = [remote(fin_a, got_a, sh_s.at[2], sh_r.at[2], s_prev), remote(fin_b, got_b, sh_s.at[3], sh_r.at[3], s_prev)]
    back[0].start()
    rb_right(K - 2).wait_recv()
    rb_left(K - 1).wait_recv()
    fin_b[...] = (sum_b[z] + rb_r[K - 2].astype(F32) + rb_l[K - 1].astype(F32)).astype(BF16)
    back[1].start()

    for copy in shift:
        copy.wait_recv()
    match = slot_match(shift_ids[...])
    back[0].wait_recv()

    def finish(got, base, width):
        rows = got.astype(F32)
        for j in range(2):
            lo = base + j * width
            piece = rows[j * SLOT:(j + 1) * SLOT].astype(BF16)
            term = lax.dot_general(match, piece, ROWS_DIM, preferred_element_type=F32)
            og_v[:, lo:lo + width] = (shift_dy[:, lo:lo + width].astype(F32) + term).astype(BF16)

    finish(got_a[...], 0, HA)
    back[1].wait_recv()
    finish(got_b[...], RA, HB)
    last = pltpu.make_async_copy(og_v, og_ref, loc.at[3])
    last.start()

    for copy in shift + back:
        copy.wait_send()
    for j, to in enumerate((y_right, y_left, y_far)):
        a1(j, to).wait_send()
        ra_y(j, to).wait_send()
    for j in range(6):
        rb_y(j).wait_send()
    for k in range(K):
        a_right(k, z).wait_send()
        b_left(k, z).wait_send()
        ra_right(k).wait_send()
        rb_left(k).wait_send()
        if k < K - 1:
            a_left(k, z).wait_send()
            b_right(k, z).wait_send()
            ra_left(k).wait_send()
            rb_right(k).wait_send()

    def sent(o, _):
        for kind in range(3):
            b_y(kind, o, y, y_right).wait_send()
        return 0

    lax.fori_loop(0, Z, sent, 0)
    for copy in outs + [last]:
        copy.wait()


def split(width):
    unit = 256
    return max(unit, (width * 3 // 8) // unit * unit)


def body(Z_AXIS, layer_input, output_grad, expert_ids, w_gate, w_up, w_down):
    Y, Z = Z_AXIS
    _, tokens, D = layer_input.shape
    hidden = w_gate.shape[2]
    CA = RA = split(D)
    K = Z // 2
    rows = Y * Z * SLOT
    CB, RB = D - CA, D - RA
    V, DMA = pltpu.VMEM, pltpu.SemaphoreType.DMA
    scratch = [
        V((tokens, D), BF16), V((tokens, D), BF16), V((D, 2 * hidden), BF16), V((D, hidden), BF16),
        V((tokens, D), BF16), V((1, tokens), jnp.int32),
        V((Z, Y, 2 * SLOT, CA), BF16), V((Z, Y, 2 * SLOT, CB), BF16),
        V((rows, D), BF16), V((rows, D), BF16), V((rows, 2 * hidden), BF16), V((rows, hidden), BF16),
        V((Z, Y * SLOT, RA), F32), V((Y, Z, SLOT, RB), F32),
        V((K, Y * SLOT, RA), BF16), V((K, Y * SLOT, RA), BF16), V((K - 1, Y * SLOT, RA), BF16), V((K - 1, Y * SLOT, RA), BF16),
        V((6, Z * SLOT, RB // 2), BF16), V((6, Z * SLOT, RB // 2), BF16), V((Z, 2 * SLOT, RB // 2), F32),
        V((K - 1, 2 * SLOT, RB // 2), BF16), V((K - 1, 2 * SLOT, RB // 2), BF16),
        V((K, 2 * SLOT, RB // 2), BF16), V((K, 2 * SLOT, RB // 2), BF16),
        V((3 + Y, 2 * SLOT, RA // 2), BF16), V((3, 2 * SLOT, RA // 2), BF16),
        V((2 * SLOT, RA // 2), BF16), V((2 * SLOT, RB // 2), BF16), V((2 * SLOT, RA // 2), BF16), V((2 * SLOT, RB // 2), BF16),
        V((tokens, D), BF16), V((D, hidden), BF16), V((D, hidden), BF16), V((D, hidden), BF16),
        DMA((5,)), DMA((4,)), DMA((4,)), DMA((3,)), DMA((3,)),
        DMA((K,)), DMA((K,)), DMA((K,)), DMA((K,)), DMA((K,)), DMA((K,)), DMA((K,)), DMA((K,)),
        DMA((3, Z)), DMA((3, Z)),
        DMA((K,)), DMA((K,)), DMA((K,)), DMA((K,)), DMA((6,)), DMA((6,)),
        DMA((K,)), DMA((K,)), DMA((K,)), DMA((K,)), DMA((3,)), DMA((3,)),
    ]
    anywhere = pl.BlockSpec(memory_space=pl.ANY)
    weight = jax.ShapeDtypeStruct((D, hidden), BF16)
    token_grad, grad_gate, grad_up, grad_down = pl.pallas_call(
        functools.partial(kernel, (Y, Z, D, CA, RA)),
        out_shape=(jax.ShapeDtypeStruct((tokens, D), BF16), weight, weight, weight),
        in_specs=[pl.BlockSpec(memory_space=pltpu.VMEM)] + [anywhere] * 5,
        out_specs=(anywhere,) * 4,
        scratch_shapes=scratch,
        compiler_params=pltpu.CompilerParams(collective_id=0, has_side_effects=True, vmem_limit_bytes=56 << 20),
    )(expert_ids, layer_input[0], output_grad[0], w_gate[0], w_up[0], w_down[0])
    return token_grad[None], grad_gate[None], grad_up[None], grad_down[None]


def solution(mesh):
    rows = P("section", ("expert", "dp"), None)
    weights = P("section", None, ("expert", "dp"))
    in_specs = (rows, rows, P("section", ("expert", "dp")), weights, weights, weights)
    out_specs = (rows, weights, weights, weights)
    size = (mesh.shape["dp"] // Z_HI, mesh.shape["expert"] * Z_HI)
    return jax.shard_map(functools.partial(body, size), mesh=mesh, in_specs=in_specs, out_specs=out_specs, check_vma=False)
```

```python
import functools

import jax
import jax.numpy as jnp
from jax import lax
from jax.experimental import pallas as pl
from jax.experimental.pallas import tpu as pltpu
from jax.sharding import PartitionSpec as P

SLOT = 8
CUTS = 4
Z_HI = 2
F32 = jnp.float32
BF16 = jnp.bfloat16
ROWS_DIM = (((0,), (0,)), ((), ()))
BACK_DIM = (((1,), (1,)), ((), ()))


def slot_match(ids):
    tokens = ids.shape[1]
    chosen = jnp.broadcast_to((ids == 0).astype(F32), (SLOT, tokens))
    before = lax.broadcasted_iota(jnp.int32, (tokens, tokens), 0)
    after = lax.broadcasted_iota(jnp.int32, (tokens, tokens), 1)
    order = (before < after).astype(F32).astype(BF16)
    within = jnp.dot(chosen.astype(BF16), order, preferred_element_type=F32)
    place = lax.broadcasted_iota(jnp.int32, (SLOT, tokens), 0).astype(F32)
    return jnp.where(within == place, chosen, 0.0).astype(BF16)


def kernel(cfg, ids_ref, x_ref, dy_ref, wg_ref, wu_ref, wd_ref, og_ref, gg_ref, gu_ref, gd_ref,
           x_v, dy_v, w_gu, w_dn, shift_dy, shift_ids, g_a, g_b, x_all, dy_all, d_gu, hid, part,
           s_r, r_r, s_l, r_l, s_y, r_y, og_v, gg_v, gu_v, gd_v,
           loc, sh_s, sh_r, a1_s, a1_r, ar_s, ar_r, al_s, al_r, br_s, br_r, bl_s, bl_r, by_s, by_r,
           rr_s, rr_r, rl_s, rl_r, ry_s, ry_r):
    Y, Z, D, CA = cfg
    CW = D // CUTS
    K = Z // 2
    n_sec, n_exp = lax.axis_size("section"), lax.axis_size("expert")
    sec, ex, dp = lax.axis_index("section"), lax.axis_index("expert"), lax.axis_index("dp")
    y, z = dp // Z_HI, lax.rem(dp, Z_HI) * n_exp + ex

    def wrap(v, n):
        return lax.rem(v + n, n)

    def at(yy, zz):
        return {"expert": lax.rem(zz, n_exp), "dp": yy * Z_HI + zz // n_exp}

    z_right, z_left = at(y, wrap(z + 1, Z)), at(y, wrap(z - 1, Z))
    y_right, y_left = at(wrap(y + 1, Y), z), at(wrap(y - 1, Y), z)
    y_far = at(wrap(y + 2, Y), z)
    s_prev, s_next = wrap(sec - 1, n_sec), wrap(sec + 1, n_sec)
    turn = (0, 1, -1, 2)
    owners = [{"section": s_prev, **at(wrap(y + t, Y), z)} for t in turn]
    givers = [{"section": s_next, **at(wrap(y - t, Y), z)} for t in turn]

    def remote(src, dst, s_sem, r_sem, to):
        return pltpu.make_async_remote_copy(
            src_ref=src, dst_ref=dst, send_sem=s_sem, recv_sem=r_sem, device_id=to, device_id_type=pl.DeviceIdType.MESH)

    barrier = pltpu.get_barrier_semaphore()
    partners = [z_right, z_left, y_right, y_left, y_far] + givers
    for to in partners:
        pl.semaphore_signal(barrier, inc=1, device_id=to, device_id_type=pl.DeviceIdType.MESH)

    half = w_gu.shape[1] // 2
    loads = [
        pltpu.make_async_copy(x_ref, x_v, loc.at[0]),
        pltpu.make_async_copy(dy_ref, dy_v, loc.at[1]),
        pltpu.make_async_copy(wg_ref, w_gu.at[:, pl.ds(0, half)], loc.at[2]),
        pltpu.make_async_copy(wu_ref, w_gu.at[:, pl.ds(half, half)], loc.at[3]),
        pltpu.make_async_copy(wd_ref, w_dn, loc.at[4]),
    ]
    for copy in loads:
        copy.start()
    match = slot_match(ids_ref[...])
    loads[0].wait()
    loads[1].wait()
    own = jnp.concatenate([
        jnp.dot(match, x_v[...], preferred_element_type=F32),
        jnp.dot(match, dy_v[...], preferred_element_type=F32)], axis=0).astype(BF16)
    g_a[z, y] = own[:, :CA]
    g_b[z, y] = own[:, CA:]
    pl.semaphore_wait(barrier, len(partners))

    def a1(j, to):
        return remote(g_a.at[z, y], g_a.at[z, y], a1_s.at[j], a1_r.at[j], to)

    def a1_in(j, yy):
        return remote(g_a.at[z, yy], g_a.at[z, yy], a1_s.at[j], a1_r.at[j], y_right)

    def a_right(k, block, j):
        ref = g_a.at[block, wrap(y + turn[j], Y)]
        return remote(ref, ref, ar_s.at[k, j], ar_r.at[k, j], z_right)

    def a_left(k, block, j):
        ref = g_a.at[block, wrap(y + turn[j], Y)]
        return remote(ref, ref, al_s.at[k, j], al_r.at[k, j], z_left)

    def b_right(k, block):
        return remote(g_b.at[block, y], g_b.at[block, y], br_s.at[k], br_r.at[k], z_right)

    def b_left(k, block):
        return remote(g_b.at[block, y], g_b.at[block, y], bl_s.at[k], bl_r.at[k], z_left)

    def b_y(kind, o, yy, to):
        block = wrap(z - o, Z)
        return remote(g_b.at[block, yy], g_b.at[block, yy], by_s.at[kind, o], by_r.at[kind, o], to)

    def spread(o):
        b_y(0, o, y, y_right).start()
        b_y(1, o, y, y_left).start()

    for j, to in enumerate((y_right, y_left, y_far)):
        a1(j, to).start()
    b_right(0, z).start()
    b_left(0, z).start()
    spread(0)
    shift = [remote(ids_ref, shift_ids, sh_s.at[0], sh_r.at[0], owners[0]), remote(dy_ref, shift_dy, sh_s.at[1], sh_r.at[1], owners[0])]
    for copy in shift:
        copy.start()
    a_right(0, z, 0).start()
    a_left(0, z, 0).start()
    for j, came in ((1, 1), (2, 0), (3, 2)):
        a1_in(came, wrap(y + turn[j], Y)).wait_recv()
        a_right(0, z, j).start()
        a_left(0, z, j).start()

    def pass_right(o):
        b_y(0, o, wrap(y - 1, Y), y_right).wait_recv()
        b_y(2, o, wrap(y - 1, Y), y_right).start()

    def pass_left(o):
        b_y(1, o, wrap(y + 1, Y), y_left).wait_recv()
        b_y(2, o, wrap(y + 1, Y), y_left).start()

    def gather_step(k, _):
        zr, zl = wrap(z - k, Z), wrap(z + k, Z)

        @pl.when(k < K)
        def _():
            b_right(k - 1, zr).wait_recv()

            @pl.when(k < K - 1)
            def _():
                b_right(k, zr).start()

            spread(k)

        b_left(k - 1, zl).wait_recv()

        @pl.when(k < K)
        def _():
            b_left(k, zl).start()

        spread(Z - k)
        for j in range(Y):
            def right(j=j):
                a_right(k - 1, zr, j).wait_recv()

                @pl.when(k < (K if j < Y // 2 else K - 1))
                def _():
                    a_right(k, zr, j).start()

            def left(j=j):
                a_left(k - 1, zl, j).wait_recv()

                @pl.when(k < (K - 1 if j < Y // 2 else K))
                def _():
                    a_left(k, zl, j).start()

            if j < Y // 2:
                right()
                pl.when(k < K)(left)
            else:
                pl.when(k < K)(right)
                left()

        pass_right(k - 1)

        @pl.when(k > 1)
        def _():
            pass_left(Z - k + 1)

        return 0

    lax.fori_loop(1, K + 1, gather_step, 0)
    pass_left(K)

    def gather_end(o, _):
        @pl.when(o < K)
        def _():
            b_y(1, o, wrap(y + 1, Y), y_left).wait_recv()

        @pl.when(o >= K)
        def _():
            b_y(0, o, wrap(y - 1, Y), y_right).wait_recv()

        b_y(2, o, wrap(y + 2, Y), y_right).wait_recv()
        return 0

    lax.fori_loop(0, Z, gather_end, 0)
    for copy in loads[2:]:
        copy.wait()

    CZ = 128 // (Y * SLOT)

    def unpack(c, _):
        rows = pl.ds(pl.multiple_of(c * (Y * SLOT), Y * SLOT), Y * SLOT)
        for ref, lo, hi in ((g_a, 0, CA), (g_b, CA, D)):
            both = ref[c].astype(F32)
            x_all[rows, lo:hi] = both[:, :SLOT].reshape(Y * SLOT, hi - lo).astype(BF16)
            dy_all[rows, lo:hi] = both[:, SLOT:].reshape(Y * SLOT, hi - lo).astype(BF16)
        return 0

    lax.fori_loop(0, Z, unpack, 0)

    def forward(c, _):
        rows = pl.ds(pl.multiple_of(c * 128, 128), 128)
        both = jnp.dot(x_all[rows, :], w_gu[...], preferred_element_type=F32)
        d_hidden = jnp.dot(dy_all[rows, :], w_dn[...], preferred_element_type=F32)
        gate, upper = both[:, :half], both[:, half:]
        sigma = jax.nn.sigmoid(gate)
        active = gate * sigma
        hid[rows, :] = (active * upper).astype(BF16)
        d_gu[rows, :half] = (d_hidden * upper * sigma * (1.0 + gate * (1.0 - sigma))).astype(BF16)
        d_gu[rows, half:] = (d_hidden * active).astype(BF16)
        for cut in range(CUTS):
            piece = lax.dot_general(
                d_gu[rows, :], w_gu[cut * CW:(cut + 1) * CW, :], BACK_DIM, preferred_element_type=F32)
            part[pl.ds(c * CZ, CZ), cut] = piece.reshape(CZ, Y * SLOT, CW)
        return 0

    lax.fori_loop(0, Z // CZ, forward, 0)

    def to_right(k, cut):
        return remote(s_r.at[k, cut], r_r.at[k, cut], rr_s.at[k, cut], rr_r.at[k, cut], z_right)

    def to_left(k, cut):
        return remote(s_l.at[k, cut], r_l.at[k, cut], rl_s.at[k, cut], rl_r.at[k, cut], z_left)

    def add_right(k, cut, got):
        value = part[wrap(z + K - k, Z), cut]
        if got:
            to_right(k - 1, cut).wait_recv()
            value = value + r_r[k - 1, cut].astype(F32)
        s_r[k, cut] = value.astype(BF16)
        to_right(k, cut).start()

    def add_left(k, cut, got):
        value = part[wrap(z - K + k, Z), cut]
        if got:
            to_left(k - 1, cut).wait_recv()
            value = value + r_l[k - 1, cut].astype(F32)
        s_l[k, cut] = value.astype(BF16)
        to_left(k, cut).start()

    WD = D // K

    def weights(j):
        cols = pl.ds(pl.multiple_of(j * WD, WD), WD)
        both = lax.dot_general(x_all[:, cols], d_gu[...], ROWS_DIM, preferred_element_type=F32).astype(BF16)
        gg_v[cols, :] = both[:, :half]
        gu_v[cols, :] = both[:, half:]
        gd_v[cols, :] = lax.dot_general(dy_all[:, cols], hid[...], ROWS_DIM, preferred_element_type=F32).astype(BF16)

    first, second = range(CUTS // 2), range(CUTS // 2, CUTS)
    for cut in first:
        add_right(0, cut, False)
    for cut in second:
        add_left(0, cut, False)
    for cut in second:
        add_right(1, cut, False)
    for cut in first:
        add_left(1, cut, False)
    weights(0)
    for a, b in zip(first, second):
        add_right(1, a, True)
        add_left(1, b, True)
    weights(1)

    def reduce_step(k, _):
        for a, b in zip(list(second) + list(first), list(first) + list(second)):
            add_right(k, a, True)
            add_left(k, b, True)
        weights(k)
        return 0

    lax.fori_loop(2, K, reduce_step, 0)
    outs = [
        pltpu.make_async_copy(gg_v, gg_ref, loc.at[0]),
        pltpu.make_async_copy(gu_v, gu_ref, loc.at[1]),
        pltpu.make_async_copy(gd_v, gd_ref, loc.at[2]),
    ]
    for copy in outs:
        copy.start()

    def to_owner(j):
        yy = wrap(y + turn[j], Y)
        return remote(s_y.at[yy], r_y.at[j], ry_s.at[j], ry_r.at[j], owners[j])

    for a, b in zip(list(second) + list(first), list(first) + list(second)):
        to_right(K - 1, a).wait_recv()
        to_left(K - 1, b).wait_recv()
    for cut in range(CUTS):
        total = part[z, cut] + r_r[K - 1, cut].astype(F32) + r_l[K - 1, cut].astype(F32)
        total = total.reshape(Y, SLOT, CW)
        total = jnp.concatenate([total[:, :, :CW // 2], total[:, :, CW // 2:]], axis=1).astype(BF16)
        s_y[:, cut] = total
    for j in (3, 1, 2, 0):
        to_owner(j).start()
    for copy in shift:
        copy.wait_recv()
    match = slot_match(shift_ids[...])
    for j in range(Y):
        to_owner(j).wait_recv()
    for cut in range(CUTS):
        rows = r_y[0, cut].astype(F32)
        for j in range(1, Y):
            rows = rows + r_y[j, cut].astype(F32)
        rows = jnp.concatenate([rows[:SLOT], rows[SLOT:]], axis=1).astype(BF16)
        term = lax.dot_general(match, rows, ROWS_DIM, preferred_element_type=F32)
        cols = slice(cut * CW, (cut + 1) * CW)
        og_v[:, cols] = (shift_dy[:, cols].astype(F32) + term).astype(BF16)
    last = pltpu.make_async_copy(og_v, og_ref, loc.at[3])
    last.start()

    for copy in shift:
        copy.wait_send()
    for j, to in enumerate((y_right, y_left, y_far)):
        a1(j, to).wait_send()
    for j in range(Y):
        to_owner(j).wait_send()

    def sent(k, _):
        for j in range(Y):
            pl.when(k < (K if j < Y // 2 else K - 1))(lambda j=j: a_right(k, z, j).wait_send())
            pl.when(k < (K - 1 if j < Y // 2 else K))(lambda j=j: a_left(k, z, j).wait_send())
        b_left(k, z).wait_send()
        pl.when(k < K - 1)(lambda: b_right(k, z).wait_send())
        for cut in range(CUTS):
            if cut in first:
                to_right(k, cut).wait_send()
                pl.when(k > 0)(lambda cut=cut: to_left(k, cut).wait_send())
            else:
                to_left(k, cut).wait_send()
                pl.when(k > 0)(lambda cut=cut: to_right(k, cut).wait_send())
        for kind in range(3):
            b_y(kind, k, y, y_right).wait_send()
            b_y(kind, K + k, y, y_right).wait_send()
        return 0

    lax.fori_loop(0, K, sent, 0)
    for copy in outs + [last]:
        copy.wait()


def handout(*refs):
    for source, target in zip(refs[:4], refs[4:]):
        target[...] = source[...]


def split(width):
    unit = 256
    return max(unit, (width * 3 // 8) // unit * unit)


def body(Z_AXIS, layer_input, output_grad, expert_ids, w_gate, w_up, w_down):
    Y, Z = Z_AXIS
    _, tokens, D = layer_input.shape
    hidden = w_gate.shape[2]
    CA = split(D)
    K = Z // 2
    rows = Y * Z * SLOT
    CB, CW = D - CA, D // CUTS
    V, DMA = pltpu.VMEM, pltpu.SemaphoreType.DMA
    scratch = [
        V((tokens, D), BF16), V((tokens, D), BF16), V((D, 2 * hidden), BF16), V((D, hidden), BF16),
        V((tokens, D), BF16), V((1, tokens), jnp.int32),
        V((Z, Y, 2 * SLOT, CA), BF16), V((Z, Y, 2 * SLOT, CB), BF16),
        V((rows, D), BF16), V((rows, D), BF16), V((rows, 2 * hidden), BF16), V((rows, hidden), BF16),
        V((Z, CUTS, Y * SLOT, CW), F32),
        *[V((K, CUTS, Y * SLOT, CW), BF16)] * 4,
        *[V((Y, CUTS, 2 * SLOT, CW // 2), BF16)] * 2,
        V((tokens, D), BF16), V((D, hidden), BF16), V((D, hidden), BF16), V((D, hidden), BF16),
        DMA((5,)), DMA((2,)), DMA((2,)), DMA((3,)), DMA((3,)),
        *[DMA((K, Y))] * 4, *[DMA((K,))] * 4, DMA((3, Z)), DMA((3, Z)),
        *[DMA((K, CUTS))] * 4, DMA((Y,)), DMA((Y,)),
    ]
    anywhere = pl.BlockSpec(memory_space=pl.ANY)
    weight = jax.ShapeDtypeStruct((D, hidden), BF16)
    token_grad, grad_gate, grad_up, grad_down = pl.pallas_call(
        functools.partial(kernel, (Y, Z, D, CA)),
        out_shape=(jax.ShapeDtypeStruct((tokens, D), BF16), weight, weight, weight),
        in_specs=[pl.BlockSpec(memory_space=pltpu.VMEM)] + [anywhere] * 5,
        out_specs=(anywhere,) * 4,
        scratch_shapes=scratch,
        compiler_params=pltpu.CompilerParams(collective_id=0, has_side_effects=True, vmem_limit_bytes=56 << 20),
    )(expert_ids, layer_input[0], output_grad[0], w_gate[0], w_up[0], w_down[0])
    steps = 4
    blocks = [pl.BlockSpec((n // steps, m), lambda i: (i, 0)) for n, m in ((tokens, D),) + ((D, hidden),) * 3]
    token_grad, grad_gate, grad_up, grad_down = pl.pallas_call(
        handout,
        grid=(steps,),
        out_shape=(jax.ShapeDtypeStruct((tokens, D), BF16), weight, weight, weight),
        in_specs=blocks,
        out_specs=blocks,
    )(token_grad, grad_gate, grad_up, grad_down)
    return token_grad[None], grad_gate[None], grad_up[None], grad_down[None]


def solution(mesh):
    rows = P("section", ("expert", "dp"), None)
    weights = P("section", None, ("expert", "dp"))
    in_specs = (rows, rows, P("section", ("expert", "dp")), weights, weights, weights)
    out_specs = (rows, weights, weights, weights)
    size = (mesh.shape["dp"] // Z_HI, mesh.shape["expert"] * Z_HI)
    return jax.shard_map(functools.partial(body, size), mesh=mesh, in_specs=in_specs, out_specs=out_specs, check_vma=False)
```

```python
import functools

import jax
import jax.numpy as jnp
from jax import lax
from jax.experimental import pallas as pl
from jax.experimental.pallas import tpu as pltpu
from jax.sharding import PartitionSpec as P

SLOT = 8
CUTS = 4
QUARTERS = 4
Z_HI = 2
F32 = jnp.float32
BF16 = jnp.bfloat16
ROWS_DIM = (((0,), (0,)), ((), ()))
BACK_DIM = (((1,), (1,)), ((), ()))


def slot_match(ids):
    tokens = ids.shape[1]
    chosen = jnp.broadcast_to((ids == 0).astype(F32), (SLOT, tokens))
    before = lax.broadcasted_iota(jnp.int32, (tokens, tokens), 0)
    after = lax.broadcasted_iota(jnp.int32, (tokens, tokens), 1)
    order = (before < after).astype(F32).astype(BF16)
    within = jnp.dot(chosen.astype(BF16), order, preferred_element_type=F32)
    place = lax.broadcasted_iota(jnp.int32, (SLOT, tokens), 0).astype(F32)
    return jnp.where(within == place, chosen, 0.0).astype(BF16)


def kernel(cfg, ids_ref, x_ref, dy_ref, wg_ref, wu_ref, wd_ref, og_ref, gg_ref, gu_ref, gd_ref,
           x_v, dy_v, w_gu, w_dn, shift_dy, shift_ids, g_a, g_b, x_all, dy_all, d_gu, hid, part,
           s_r, r_r, s_l, r_l, s_y, r_y, og_v, gg_v, gu_v, gd_v,
           loc, sh_s, sh_r, a1_s, a1_r, ar_s, ar_r, al_s, al_r, br_s, br_r, bl_s, bl_r, by_s, by_r,
           rr_s, rr_r, rl_s, rl_r, ry_s, ry_r):
    Y, Z, D, CA = cfg
    CW = D // CUTS
    K = Z // 2
    n_sec, n_exp = lax.axis_size("section"), lax.axis_size("expert")
    sec, ex, dp = lax.axis_index("section"), lax.axis_index("expert"), lax.axis_index("dp")
    y, z = dp // Z_HI, lax.rem(dp, Z_HI) * n_exp + ex

    def wrap(v, n):
        return lax.rem(v + n, n)

    def at(yy, zz):
        return {"expert": lax.rem(zz, n_exp), "dp": yy * Z_HI + zz // n_exp}

    z_right, z_left = at(y, wrap(z + 1, Z)), at(y, wrap(z - 1, Z))
    y_right, y_left = at(wrap(y + 1, Y), z), at(wrap(y - 1, Y), z)
    y_far = at(wrap(y + 2, Y), z)
    s_prev, s_next = wrap(sec - 1, n_sec), wrap(sec + 1, n_sec)
    turn = (0, 1, -1, 2)
    owners = [{"section": s_prev, **at(wrap(y + t, Y), z)} for t in turn]
    givers = [{"section": s_next, **at(wrap(y - t, Y), z)} for t in turn]

    def remote(src, dst, s_sem, r_sem, to):
        return pltpu.make_async_remote_copy(
            src_ref=src, dst_ref=dst, send_sem=s_sem, recv_sem=r_sem, device_id=to, device_id_type=pl.DeviceIdType.MESH)

    barrier = pltpu.get_barrier_semaphore()
    partners = [z_right, z_left, y_right, y_left, y_far] + givers
    for to in partners:
        pl.semaphore_signal(barrier, inc=1, device_id=to, device_id_type=pl.DeviceIdType.MESH)

    half = w_gu.shape[1] // 2
    loads = [
        pltpu.make_async_copy(x_ref, x_v, loc.at[0]),
        pltpu.make_async_copy(dy_ref, dy_v, loc.at[1]),
        pltpu.make_async_copy(wg_ref, w_gu.at[:, pl.ds(0, half)], loc.at[2]),
        pltpu.make_async_copy(wu_ref, w_gu.at[:, pl.ds(half, half)], loc.at[3]),
        pltpu.make_async_copy(wd_ref, w_dn, loc.at[4]),
    ]
    for copy in loads:
        copy.start()
    match = slot_match(ids_ref[...])
    loads[0].wait()
    loads[1].wait()
    own = jnp.concatenate([
        jnp.dot(match, x_v[...], preferred_element_type=F32),
        jnp.dot(match, dy_v[...], preferred_element_type=F32)], axis=0).astype(BF16)
    g_a[z, y] = own[:, :CA]
    g_b[z, y] = own[:, CA:]
    pl.semaphore_wait(barrier, len(partners))

    def a1(j, to):
        return remote(g_a.at[z, y], g_a.at[z, y], a1_s.at[j], a1_r.at[j], to)

    def a1_in(j, yy):
        return remote(g_a.at[z, yy], g_a.at[z, yy], a1_s.at[j], a1_r.at[j], y_right)

    def a_right(k, block, j):
        ref = g_a.at[block, wrap(y + turn[j], Y)]
        return remote(ref, ref, ar_s.at[k, j], ar_r.at[k, j], z_right)

    def a_left(k, block, j):
        ref = g_a.at[block, wrap(y + turn[j], Y)]
        return remote(ref, ref, al_s.at[k, j], al_r.at[k, j], z_left)

    def b_right(k, block):
        return remote(g_b.at[block, y], g_b.at[block, y], br_s.at[k], br_r.at[k], z_right)

    def b_left(k, block):
        return remote(g_b.at[block, y], g_b.at[block, y], bl_s.at[k], bl_r.at[k], z_left)

    def b_y(kind, o, yy, to):
        block = wrap(z - o, Z)
        return remote(g_b.at[block, yy], g_b.at[block, yy], by_s.at[kind, o], by_r.at[kind, o], to)

    def spread(o):
        b_y(0, o, y, y_right).start()
        b_y(1, o, y, y_left).start()

    for j, to in enumerate((y_right, y_left, y_far)):
        a1(j, to).start()
    b_right(0, z).start()
    b_left(0, z).start()
    spread(0)
    shift = [remote(ids_ref, shift_ids, sh_s.at[0], sh_r.at[0], owners[0]), remote(dy_ref, shift_dy, sh_s.at[1], sh_r.at[1], owners[0])]
    for copy in shift:
        copy.start()
    a_right(0, z, 0).start()
    a_left(0, z, 0).start()
    for j, came in ((1, 1), (2, 0), (3, 2)):
        a1_in(came, wrap(y + turn[j], Y)).wait_recv()
        a_right(0, z, j).start()
        a_left(0, z, j).start()

    def pass_right(o):
        b_y(0, o, wrap(y - 1, Y), y_right).wait_recv()
        b_y(2, o, wrap(y - 1, Y), y_right).start()

    def pass_left(o):
        b_y(1, o, wrap(y + 1, Y), y_left).wait_recv()
        b_y(2, o, wrap(y + 1, Y), y_left).start()

    CZ = Z // QUARTERS
    QR = CZ * Y * SLOT

    def quarter(i):
        rows = pl.ds(pl.multiple_of(i * QR, QR), QR)

        def unpack(n, _):
            place = i * CZ + n
            away = lax.rem(place, 2) * (place + 1) // 2 - (1 - lax.rem(place, 2)) * (place // 2)
            block = wrap(z + away, Z)
            o = wrap(-away, Z)

            @pl.when(o < K)
            def _():
                b_y(1, o, wrap(y + 1, Y), y_left).wait_recv()

            @pl.when(o >= K)
            def _():
                b_y(0, o, wrap(y - 1, Y), y_right).wait_recv()

            b_y(2, o, wrap(y + 2, Y), y_right).wait_recv()
            here = pl.ds(pl.multiple_of(place * (Y * SLOT), Y * SLOT), Y * SLOT)
            for ref, lo, hi in ((g_a, 0, CA), (g_b, CA, D)):
                both = ref[block].astype(F32)
                x_all[here, lo:hi] = both[:, :SLOT].reshape(Y * SLOT, hi - lo).astype(BF16)
                dy_all[here, lo:hi] = both[:, SLOT:].reshape(Y * SLOT, hi - lo).astype(BF16)
            return 0

        lax.fori_loop(0, CZ, unpack, 0)
        both = jnp.dot(x_all[rows, :], w_gu[...], preferred_element_type=F32)
        d_hidden = jnp.dot(dy_all[rows, :], w_dn[...], preferred_element_type=F32)
        gate, upper = both[:, :half], both[:, half:]
        sigma = jax.nn.sigmoid(gate)
        active = gate * sigma
        hid[rows, :] = (active * upper).astype(BF16)
        d_gu[rows, :half] = (d_hidden * upper * sigma * (1.0 + gate * (1.0 - sigma))).astype(BF16)
        d_gu[rows, half:] = (d_hidden * active).astype(BF16)
        for cut in range(CUTS):
            piece = lax.dot_general(
                d_gu[rows, :], w_gu[cut * CW:(cut + 1) * CW, :], BACK_DIM, preferred_element_type=F32)
            part[pl.ds(i * CZ, CZ), cut] = piece.reshape(CZ, Y * SLOT, CW)

    def gather_step(k, _):
        zr, zl = wrap(z - k, Z), wrap(z + k, Z)

        @pl.when(k < K)
        def _():
            b_right(k - 1, zr).wait_recv()

            @pl.when(k < K - 1)
            def _():
                b_right(k, zr).start()

            spread(k)

        b_left(k - 1, zl).wait_recv()

        @pl.when(k < K)
        def _():
            b_left(k, zl).start()

        spread(Z - k)
        for j in range(Y):
            def right(j=j):
                a_right(k - 1, zr, j).wait_recv()

                @pl.when(k < (K if j < Y // 2 else K - 1))
                def _():
                    a_right(k, zr, j).start()

            def left(j=j):
                a_left(k - 1, zl, j).wait_recv()

                @pl.when(k < (K - 1 if j < Y // 2 else K))
                def _():
                    a_left(k, zl, j).start()

            if j < Y // 2:
                right()
                pl.when(k < K)(left)
            else:
                pl.when(k < K)(right)
                left()

        pass_right(k - 1)

        @pl.when(k > 1)
        def _():
            pass_left(Z - k + 1)

        early = K // 2 + 1

        if K == 2 * QUARTERS:
            @pl.when((k >= early) & (lax.rem(k - early, 2) == 0) & (k < K))
            def _():
                quarter((k - early) // 2)

        return 0

    for copy in loads[2:]:
        copy.wait()
    lax.fori_loop(1, K + 1, gather_step, 0)
    pass_left(K)
    if K != 2 * QUARTERS:
        for i in range(QUARTERS - 1):
            quarter(i)

    quarter(QUARTERS - 1)

    def to_right(k, cut):
        return remote(s_r.at[k, cut], r_r.at[k, cut], rr_s.at[k, cut], rr_r.at[k, cut], z_right)

    def to_left(k, cut):
        return remote(s_l.at[k, cut], r_l.at[k, cut], rl_s.at[k, cut], rl_r.at[k, cut], z_left)

    def add_right(k, cut, got):
        value = part[2 * (K - k) - 1, cut]
        if got:
            to_right(k - 1, cut).wait_recv()
            value = value + r_r[k - 1, cut].astype(F32)
        s_r[k, cut] = value.astype(BF16)
        to_right(k, cut).start()

    def add_left(k, cut, got):
        value = part[2 * (K - k) - (1 if isinstance(k, int) and k == 0 else 0), cut]
        if got:
            to_left(k - 1, cut).wait_recv()
            value = value + r_l[k - 1, cut].astype(F32)
        s_l[k, cut] = value.astype(BF16)
        to_left(k, cut).start()

    WD = D // K

    def weights(j):
        cols = pl.ds(pl.multiple_of(j * WD, WD), WD)
        both = lax.dot_general(x_all[:, cols], d_gu[...], ROWS_DIM, preferred_element_type=F32).astype(BF16)
        gg_v[cols, :] = both[:, :half]
        gu_v[cols, :] = both[:, half:]
        gd_v[cols, :] = lax.dot_general(dy_all[:, cols], hid[...], ROWS_DIM, preferred_element_type=F32).astype(BF16)

    first, second = range(CUTS // 2), range(CUTS // 2, CUTS)
    for cut in first:
        add_right(0, cut, False)
    for cut in second:
        add_left(0, cut, False)
    for cut in second:
        add_right(1, cut, False)
    for cut in first:
        add_left(1, cut, False)
    if K == 2 * QUARTERS:
        quarter(QUARTERS - 2)
    for a, b in zip(first, second):
        add_right(1, a, True)
        add_left(1, b, True)
    weights(0)
    weights(1)

    def reduce_step(k, _):
        for a, b in zip(list(second) + list(first), list(first) + list(second)):
            add_right(k, a, True)
            add_left(k, b, True)
        weights(k)
        return 0

    lax.fori_loop(2, K, reduce_step, 0)
    outs = [
        pltpu.make_async_copy(gg_v, gg_ref, loc.at[0]),
        pltpu.make_async_copy(gu_v, gu_ref, loc.at[1]),
        pltpu.make_async_copy(gd_v, gd_ref, loc.at[2]),
    ]
    for copy in outs:
        copy.start()

    def to_owner(j):
        yy = wrap(y + turn[j], Y)
        return remote(s_y.at[yy], r_y.at[j], ry_s.at[j], ry_r.at[j], owners[j])

    for a, b in zip(list(second) + list(first), list(first) + list(second)):
        to_right(K - 1, a).wait_recv()
        to_left(K - 1, b).wait_recv()
    for cut in range(CUTS):
        total = part[0, cut] + r_r[K - 1, cut].astype(F32) + r_l[K - 1, cut].astype(F32)
        total = total.reshape(Y, SLOT, CW)
        total = jnp.concatenate([total[:, :, :CW // 2], total[:, :, CW // 2:]], axis=1).astype(BF16)
        s_y[:, cut] = total
    for j in (3, 1, 2, 0):
        to_owner(j).start()
    for copy in shift:
        copy.wait_recv()
    match = slot_match(shift_ids[...])
    for j in range(Y):
        to_owner(j).wait_recv()
    for cut in range(CUTS):
        rows = r_y[0, cut].astype(F32)
        for j in range(1, Y):
            rows = rows + r_y[j, cut].astype(F32)
        rows = jnp.concatenate([rows[:SLOT], rows[SLOT:]], axis=1).astype(BF16)
        term = lax.dot_general(match, rows, ROWS_DIM, preferred_element_type=F32)
        cols = slice(cut * CW, (cut + 1) * CW)
        og_v[:, cols] = (shift_dy[:, cols].astype(F32) + term).astype(BF16)
    last = pltpu.make_async_copy(og_v, og_ref, loc.at[3])
    last.start()

    for copy in shift:
        copy.wait_send()
    for j, to in enumerate((y_right, y_left, y_far)):
        a1(j, to).wait_send()
    for j in range(Y):
        to_owner(j).wait_send()

    def sent(k, _):
        for j in range(Y):
            pl.when(k < (K if j < Y // 2 else K - 1))(lambda j=j: a_right(k, z, j).wait_send())
            pl.when(k < (K - 1 if j < Y // 2 else K))(lambda j=j: a_left(k, z, j).wait_send())
        b_left(k, z).wait_send()
        pl.when(k < K - 1)(lambda: b_right(k, z).wait_send())
        for cut in range(CUTS):
            if cut in first:
                to_right(k, cut).wait_send()
                pl.when(k > 0)(lambda cut=cut: to_left(k, cut).wait_send())
            else:
                to_left(k, cut).wait_send()
                pl.when(k > 0)(lambda cut=cut: to_right(k, cut).wait_send())
        for kind in range(3):
            b_y(kind, k, y, y_right).wait_send()
            b_y(kind, K + k, y, y_right).wait_send()
        return 0

    lax.fori_loop(0, K, sent, 0)
    for copy in outs + [last]:
        copy.wait()


def handout(*refs):
    for source, target in zip(refs[:4], refs[4:]):
        target[...] = source[...]


def split(width):
    unit = 256
    return max(unit, (width * 3 // 8) // unit * unit)


def body(Z_AXIS, layer_input, output_grad, expert_ids, w_gate, w_up, w_down):
    Y, Z = Z_AXIS
    _, tokens, D = layer_input.shape
    hidden = w_gate.shape[2]
    CA = split(D)
    K = Z // 2
    rows = Y * Z * SLOT
    CB, CW = D - CA, D // CUTS
    V, DMA = pltpu.VMEM, pltpu.SemaphoreType.DMA
    scratch = [
        V((tokens, D), BF16), V((tokens, D), BF16), V((D, 2 * hidden), BF16), V((D, hidden), BF16),
        V((tokens, D), BF16), V((1, tokens), jnp.int32),
        V((Z, Y, 2 * SLOT, CA), BF16), V((Z, Y, 2 * SLOT, CB), BF16),
        V((rows, D), BF16), V((rows, D), BF16), V((rows, 2 * hidden), BF16), V((rows, hidden), BF16),
        V((Z, CUTS, Y * SLOT, CW), F32),
        *[V((K, CUTS, Y * SLOT, CW), BF16)] * 4,
        *[V((Y, CUTS, 2 * SLOT, CW // 2), BF16)] * 2,
        V((tokens, D), BF16), V((D, hidden), BF16), V((D, hidden), BF16), V((D, hidden), BF16),
        DMA((5,)), DMA((2,)), DMA((2,)), DMA((3,)), DMA((3,)),
        *[DMA((K, Y))] * 4, *[DMA((K,))] * 4, DMA((3, Z)), DMA((3, Z)),
        *[DMA((K, CUTS))] * 4, DMA((Y,)), DMA((Y,)),
    ]
    anywhere = pl.BlockSpec(memory_space=pl.ANY)
    weight = jax.ShapeDtypeStruct((D, hidden), BF16)
    token_grad, grad_gate, grad_up, grad_down = pl.pallas_call(
        functools.partial(kernel, (Y, Z, D, CA)),
        out_shape=(jax.ShapeDtypeStruct((tokens, D), BF16), weight, weight, weight),
        in_specs=[pl.BlockSpec(memory_space=pltpu.VMEM)] + [anywhere] * 5,
        out_specs=(anywhere,) * 4,
        scratch_shapes=scratch,
        compiler_params=pltpu.CompilerParams(collective_id=0, has_side_effects=True, vmem_limit_bytes=56 << 20),
    )(expert_ids, layer_input[0], output_grad[0], w_gate[0], w_up[0], w_down[0])
    steps = 4
    blocks = [pl.BlockSpec((n // steps, m), lambda i: (i, 0)) for n, m in ((tokens, D),) + ((D, hidden),) * 3]
    token_grad, grad_gate, grad_up, grad_down = pl.pallas_call(
        handout,
        grid=(steps,),
        out_shape=(jax.ShapeDtypeStruct((tokens, D), BF16), weight, weight, weight),
        in_specs=blocks,
        out_specs=blocks,
    )(token_grad, grad_gate, grad_up, grad_down)
    return token_grad[None], grad_gate[None], grad_up[None], grad_down[None]


def solution(mesh):
    rows = P("section", ("expert", "dp"), None)
    weights = P("section", None, ("expert", "dp"))
    in_specs = (rows, rows, P("section", ("expert", "dp")), weights, weights, weights)
    out_specs = (rows, weights, weights, weights)
    size = (mesh.shape["dp"] // Z_HI, mesh.shape["expert"] * Z_HI)
    return jax.shard_map(functools.partial(body, size), mesh=mesh, in_specs=in_specs, out_specs=out_specs, check_vma=False)
```

```python
import functools

import jax
import jax.numpy as jnp
from jax import lax
from jax.experimental import pallas as pl
from jax.experimental.pallas import tpu as pltpu
from jax.sharding import PartitionSpec as P

SLOT = 8
CUTS = 4
RING = 3
QUARTERS = 4
Z_HI = 2
F32 = jnp.float32
BF16 = jnp.bfloat16
ROWS_DIM = (((0,), (0,)), ((), ()))
BACK_DIM = (((1,), (1,)), ((), ()))


def slot_match(ids):
    tokens = ids.shape[1]
    chosen = jnp.broadcast_to((ids == 0).astype(F32), (SLOT, tokens))
    before = lax.broadcasted_iota(jnp.int32, (tokens, tokens), 0)
    after = lax.broadcasted_iota(jnp.int32, (tokens, tokens), 1)
    order = (before < after).astype(F32).astype(BF16)
    within = jnp.dot(chosen.astype(BF16), order, preferred_element_type=F32)
    place = lax.broadcasted_iota(jnp.int32, (SLOT, tokens), 0).astype(F32)
    return jnp.where(within == place, chosen, 0.0).astype(BF16)


def kernel(cfg, ids_ref, x_ref, dy_ref, wg_ref, wu_ref, wd_ref, og_ref, gg_ref, gu_ref, gd_ref,
           x_v, dy_v, w_gu, w_dn, shift_dy, shift_ids, g_a, g_b, x_all, dy_all, d_gu, hid, part, part_y,
           s_r, r_r, s_l, r_l, s_y, r_y, s_q, r_q, s_br, r_br, s_bl, r_bl, s_f, r_f, og_v, gg_v, gu_v, gd_v,
           loc, sh_s, sh_r, a1_s, a1_r, ar_s, ar_r, al_s, al_r, br_s, br_r, bl_s, bl_r, by_s, by_r,
           rr_s, rr_r, rl_s, rl_r, ry_s, ry_r, q_s, q_r, tr_s, tr_r, tl_s, tl_r, f_s, f_r):
    Y, Z, D, CA = cfg
    CW = D // CUTS
    K = Z // 2
    n_sec, n_exp = lax.axis_size("section"), lax.axis_size("expert")
    sec, ex, dp = lax.axis_index("section"), lax.axis_index("expert"), lax.axis_index("dp")
    y, z = dp // Z_HI, lax.rem(dp, Z_HI) * n_exp + ex

    def wrap(v, n):
        return lax.rem(v + n, n)

    def at(yy, zz):
        return {"expert": lax.rem(zz, n_exp), "dp": yy * Z_HI + zz // n_exp}

    z_right, z_left = at(y, wrap(z + 1, Z)), at(y, wrap(z - 1, Z))
    y_right, y_left = at(wrap(y + 1, Y), z), at(wrap(y - 1, Y), z)
    y_far = at(wrap(y + 2, Y), z)
    s_prev, s_next = wrap(sec - 1, n_sec), wrap(sec + 1, n_sec)
    turn = (0, 1, -1, 2)
    owners = [{"section": s_prev, **at(wrap(y + t, Y), z)} for t in turn]
    givers = [{"section": s_next, **at(wrap(y - t, Y), z)} for t in turn]

    def remote(src, dst, s_sem, r_sem, to):
        return pltpu.make_async_remote_copy(
            src_ref=src, dst_ref=dst, send_sem=s_sem, recv_sem=r_sem, device_id=to, device_id_type=pl.DeviceIdType.MESH)

    barrier = pltpu.get_barrier_semaphore()
    partners = [z_right, z_left, y_right, y_left, y_far] + givers
    for to in partners:
        pl.semaphore_signal(barrier, inc=1, device_id=to, device_id_type=pl.DeviceIdType.MESH)

    half = w_gu.shape[1] // 2
    loads = [
        pltpu.make_async_copy(x_ref, x_v, loc.at[0]),
        pltpu.make_async_copy(dy_ref, dy_v, loc.at[1]),
        pltpu.make_async_copy(wg_ref, w_gu.at[:, pl.ds(0, half)], loc.at[2]),
        pltpu.make_async_copy(wu_ref, w_gu.at[:, pl.ds(half, half)], loc.at[3]),
        pltpu.make_async_copy(wd_ref, w_dn, loc.at[4]),
    ]
    for copy in loads:
        copy.start()
    match = slot_match(ids_ref[...])
    loads[0].wait()
    loads[1].wait()
    own = jnp.concatenate([
        jnp.dot(match, x_v[...], preferred_element_type=F32),
        jnp.dot(match, dy_v[...], preferred_element_type=F32)], axis=0).astype(BF16)
    g_a[z, y] = own[:, :CA]
    g_b[z, y] = own[:, CA:]
    pl.semaphore_wait(barrier, len(partners))

    def a1(j, to):
        return remote(g_a.at[z, y], g_a.at[z, y], a1_s.at[j], a1_r.at[j], to)

    def a1_in(j, yy):
        return remote(g_a.at[z, yy], g_a.at[z, yy], a1_s.at[j], a1_r.at[j], y_right)

    def a_right(k, block, j):
        ref = g_a.at[block, wrap(y + turn[j], Y)]
        return remote(ref, ref, ar_s.at[k, j], ar_r.at[k, j], z_right)

    def a_left(k, block, j):
        ref = g_a.at[block, wrap(y + turn[j], Y)]
        return remote(ref, ref, al_s.at[k, j], al_r.at[k, j], z_left)

    def b_right(k, block):
        return remote(g_b.at[block, y], g_b.at[block, y], br_s.at[k], br_r.at[k], z_right)

    def b_left(k, block):
        return remote(g_b.at[block, y], g_b.at[block, y], bl_s.at[k], bl_r.at[k], z_left)

    def b_y(kind, o, yy, to):
        block = wrap(z - o, Z)
        return remote(g_b.at[block, yy], g_b.at[block, yy], by_s.at[kind, o], by_r.at[kind, o], to)

    def spread(o):
        b_y(0, o, y, y_right).start()
        b_y(1, o, y, y_left).start()

    for j, to in enumerate((y_right, y_left, y_far)):
        a1(j, to).start()
    b_right(0, z).start()
    b_left(0, z).start()
    spread(0)
    shift = [remote(ids_ref, shift_ids, sh_s.at[0], sh_r.at[0], owners[0]), remote(dy_ref, shift_dy, sh_s.at[1], sh_r.at[1], owners[0])]
    for copy in shift:
        copy.start()
    a_right(0, z, 0).start()
    a_left(0, z, 0).start()
    for j, came in ((1, 1), (2, 0), (3, 2)):
        a1_in(came, wrap(y + turn[j], Y)).wait_recv()
        a_right(0, z, j).start()
        a_left(0, z, j).start()

    def pass_right(o):
        b_y(0, o, wrap(y - 1, Y), y_right).wait_recv()
        b_y(2, o, wrap(y - 1, Y), y_right).start()

    def pass_left(o):
        b_y(1, o, wrap(y + 1, Y), y_left).wait_recv()
        b_y(2, o, wrap(y + 1, Y), y_left).start()

    CZ = Z // QUARTERS
    QR = CZ * Y * SLOT

    def swap(i, j):
        return remote(s_q.at[i, j], r_q.at[i, j], q_s.at[i, j], q_r.at[i, j], (y_right, y_left, y_far)[j])

    def swapped(i):
        for j in range(Y - 1):
            swap(i, j).wait_recv()

    def quarter(i):
        rows = pl.ds(pl.multiple_of(i * QR, QR), QR)

        def unpack(n, _):
            place = i * CZ + n
            away = lax.rem(place, 2) * (place + 1) // 2 - (1 - lax.rem(place, 2)) * (place // 2)
            block = wrap(z + away, Z)
            o = wrap(-away, Z)

            @pl.when(o < K)
            def _():
                b_y(1, o, wrap(y + 1, Y), y_left).wait_recv()

            @pl.when(o >= K)
            def _():
                b_y(0, o, wrap(y - 1, Y), y_right).wait_recv()

            b_y(2, o, wrap(y + 2, Y), y_right).wait_recv()
            here = pl.ds(pl.multiple_of(place * (Y * SLOT), Y * SLOT), Y * SLOT)
            for ref, lo, hi in ((g_a, 0, CA), (g_b, CA, D)):
                both = ref[block].astype(F32)
                x_all[here, lo:hi] = both[:, :SLOT].reshape(Y * SLOT, hi - lo).astype(BF16)
                dy_all[here, lo:hi] = both[:, SLOT:].reshape(Y * SLOT, hi - lo).astype(BF16)
            return 0

        lax.fori_loop(0, CZ, unpack, 0)
        both = jnp.dot(x_all[rows, :], w_gu[...], preferred_element_type=F32)
        d_hidden = jnp.dot(dy_all[rows, :], w_dn[...], preferred_element_type=F32)
        gate, upper = both[:, :half], both[:, half:]
        sigma = jax.nn.sigmoid(gate)
        active = gate * sigma
        hid[rows, :] = (active * upper).astype(BF16)
        d_gu[rows, :half] = (d_hidden * upper * sigma * (1.0 + gate * (1.0 - sigma))).astype(BF16)
        d_gu[rows, half:] = (d_hidden * active).astype(BF16)
        for cut in range(CUTS - 1, -1, -1):
            piece = lax.dot_general(
                d_gu[rows, :], w_gu[cut * CW:(cut + 1) * CW, :], BACK_DIM, preferred_element_type=F32)
            if cut < RING:
                part[pl.ds(i * CZ, CZ), cut] = piece.reshape(CZ, Y * SLOT, CW)
            else:
                piece = piece.reshape(CZ, Y, SLOT, CW)
                part_y[pl.ds(i * CZ, CZ)] = jnp.concatenate([piece[..., :CW // 2], piece[..., CW // 2:]], axis=2)
                for j in (2, 0, 1):
                    yy = wrap(y + turn[j + 1], Y)
                    for n in range(CZ):
                        s_q[i, j, n] = part_y[i * CZ + n, yy].astype(BF16)
                    swap(i, j).start()

    def gather_step(k, _):
        zr, zl = wrap(z - k, Z), wrap(z + k, Z)

        @pl.when(k < K)
        def _():
            b_right(k - 1, zr).wait_recv()

            @pl.when(k < K - 1)
            def _():
                b_right(k, zr).start()

            spread(k)

        b_left(k - 1, zl).wait_recv()

        @pl.when(k < K)
        def _():
            b_left(k, zl).start()

        spread(Z - k)
        for j in range(Y):
            def right(j=j):
                a_right(k - 1, zr, j).wait_recv()

                @pl.when(k < (K if j < Y // 2 else K - 1))
                def _():
                    a_right(k, zr, j).start()

            def left(j=j):
                a_left(k - 1, zl, j).wait_recv()

                @pl.when(k < (K - 1 if j < Y // 2 else K))
                def _():
                    a_left(k, zl, j).start()

            if j < Y // 2:
                right()
                pl.when(k < K)(left)
            else:
                pl.when(k < K)(right)
                left()

        pass_right(k - 1)

        @pl.when(k > 1)
        def _():
            pass_left(Z - k + 1)

        early = K // 2 + 1

        if K == 2 * QUARTERS:
            @pl.when((k >= early) & (lax.rem(k - early, 2) == 0) & (k < K))
            def _():
                quarter((k - early) // 2)

        return 0

    for copy in loads[2:]:
        copy.wait()
    lax.fori_loop(1, K + 1, gather_step, 0)
    pass_left(K)
    if K != 2 * QUARTERS:
        for i in range(QUARTERS - 1):
            quarter(i)

    quarter(QUARTERS - 1)

    def to_right(k, cut):
        return remote(s_r.at[k, cut], r_r.at[k, cut], rr_s.at[k, cut], rr_r.at[k, cut], z_right)

    def to_left(k, cut):
        return remote(s_l.at[k, cut], r_l.at[k, cut], rl_s.at[k, cut], rl_r.at[k, cut], z_left)

    def add_right(k, cut, got):
        value = part[2 * (K - k) - 1, cut]
        if got:
            to_right(k - 1, cut).wait_recv()
            value = value + r_r[k - 1, cut].astype(F32)
        s_r[k, cut] = value.astype(BF16)
        to_right(k, cut).start()

    def add_left(k, cut, got):
        value = part[2 * (K - k) - (1 if isinstance(k, int) and k == 0 else 0), cut]
        if got:
            to_left(k - 1, cut).wait_recv()
            value = value + r_l[k - 1, cut].astype(F32)
        s_l[k, cut] = value.astype(BF16)
        to_left(k, cut).start()

    WD = D // K

    def weights(j):
        cols = pl.ds(pl.multiple_of(j * WD, WD), WD)
        both = lax.dot_general(x_all[:, cols], d_gu[...], ROWS_DIM, preferred_element_type=F32).astype(BF16)
        gg_v[cols, :] = both[:, :half]
        gu_v[cols, :] = both[:, half:]
        gd_v[cols, :] = lax.dot_general(dy_all[:, cols], hid[...], ROWS_DIM, preferred_element_type=F32).astype(BF16)

    def tall_right(k):
        return remote(s_br.at[k], r_br.at[k], tr_s.at[k], tr_r.at[k], z_right)

    def tall_left(k):
        return remote(s_bl.at[k], r_bl.at[k], tl_s.at[k], tl_r.at[k], z_left)

    def over_y(place):
        value = part_y[place, y]
        for j in range(Y - 1):
            value = value + r_q[place // CZ, j, lax.rem(place, CZ)].astype(F32)
        return value

    def add_tall(k, right, left):
        if right is not None:
            value = over_y(2 * (K - k) - 1)
            if right:
                tall_right(k - 1).wait_recv()
                value = value + r_br[k - 1].astype(F32)
            s_br[k] = value.astype(BF16)
            tall_right(k).start()
        value = over_y(2 * (K - k) - (1 if isinstance(k, int) and k == 0 else 0))
        if left:
            tall_left(k - 1).wait_recv()
            value = value + r_bl[k - 1].astype(F32)
        s_bl[k] = value.astype(BF16)
        tall_left(k).start()

    first, second = range((RING + 1) // 2), range((RING + 1) // 2, RING)
    for cut in first:
        add_right(0, cut, False)
    for cut in second:
        add_left(0, cut, False)
    for cut in second:
        add_right(1, cut, False)
    for cut in first:
        add_left(1, cut, False)
    swapped(QUARTERS - 1)
    if K != 2 * QUARTERS:
        for i in range(QUARTERS - 1):
            swapped(i)
    add_tall(0, None, False)
    if K == 2 * QUARTERS:
        quarter(QUARTERS - 2)
    for cut in first:
        add_right(1, cut, True)
    for cut in second:
        add_left(1, cut, True)
    add_tall(1, False, True)
    weights(0)
    weights(1)

    def reduce_step(k, _):
        for cut in range(RING):
            add_right(k, RING - 1 - cut, True)
            add_left(k, cut, True)
        if K == 2 * QUARTERS:
            pl.when(lax.rem(k, 2) == 0)(lambda: swapped((K - k) // 2 - 1))
        add_tall(k, True, True)
        weights(k)
        return 0

    lax.fori_loop(2, K, reduce_step, 0)
    outs = [
        pltpu.make_async_copy(gg_v, gg_ref, loc.at[0]),
        pltpu.make_async_copy(gu_v, gu_ref, loc.at[1]),
        pltpu.make_async_copy(gd_v, gd_ref, loc.at[2]),
    ]
    for copy in outs:
        copy.start()

    def to_owner(j):
        yy = wrap(y + turn[j], Y)
        return remote(s_y.at[yy], r_y.at[j], ry_s.at[j], ry_r.at[j], owners[j])

    for cut in range(RING):
        to_right(K - 1, RING - 1 - cut).wait_recv()
        to_left(K - 1, cut).wait_recv()
    for cut in range(RING):
        total = part[0, cut] + r_r[K - 1, cut].astype(F32) + r_l[K - 1, cut].astype(F32)
        total = total.reshape(Y, SLOT, CW)
        total = jnp.concatenate([total[:, :, :CW // 2], total[:, :, CW // 2:]], axis=1).astype(BF16)
        s_y[:, cut] = total
    for j in (3, 1, 2, 0):
        to_owner(j).start()
    tall_right(K - 1).wait_recv()
    tall_left(K - 1).wait_recv()
    s_f[...] = (over_y(0) + r_br[K - 1].astype(F32) + r_bl[K - 1].astype(F32)).astype(BF16)
    whole = remote(s_f, r_f, f_s.at[0], f_r.at[0], owners[0])
    whole.start()
    for copy in shift:
        copy.wait_recv()
    match = slot_match(shift_ids[...])
    for j in range(Y):
        to_owner(j).wait_recv()
    for cut in range(CUTS):
        if cut < RING:
            rows = r_y[0, cut].astype(F32)
            for j in range(1, Y):
                rows = rows + r_y[j, cut].astype(F32)
        else:
            whole.wait_recv()
            rows = r_f[...].astype(F32)
        rows = jnp.concatenate([rows[:SLOT], rows[SLOT:]], axis=1).astype(BF16)
        term = lax.dot_general(match, rows, ROWS_DIM, preferred_element_type=F32)
        cols = slice(cut * CW, (cut + 1) * CW)
        og_v[:, cols] = (shift_dy[:, cols].astype(F32) + term).astype(BF16)
    last = pltpu.make_async_copy(og_v, og_ref, loc.at[3])
    last.start()

    for copy in shift:
        copy.wait_send()
    for j, to in enumerate((y_right, y_left, y_far)):
        a1(j, to).wait_send()
    for j in range(Y):
        to_owner(j).wait_send()
    whole.wait_send()
    for i in range(QUARTERS):
        for j in range(Y - 1):
            swap(i, j).wait_send()

    def sent(k, _):
        for j in range(Y):
            pl.when(k < (K if j < Y // 2 else K - 1))(lambda j=j: a_right(k, z, j).wait_send())
            pl.when(k < (K - 1 if j < Y // 2 else K))(lambda j=j: a_left(k, z, j).wait_send())
        b_left(k, z).wait_send()
        pl.when(k < K - 1)(lambda: b_right(k, z).wait_send())
        tall_left(k).wait_send()
        pl.when(k > 0)(lambda: tall_right(k).wait_send())
        for cut in range(RING):
            if cut in first:
                to_right(k, cut).wait_send()
                pl.when(k > 0)(lambda cut=cut: to_left(k, cut).wait_send())
            else:
                to_left(k, cut).wait_send()
                pl.when(k > 0)(lambda cut=cut: to_right(k, cut).wait_send())
        for kind in range(3):
            b_y(kind, k, y, y_right).wait_send()
            b_y(kind, K + k, y, y_right).wait_send()
        return 0

    lax.fori_loop(0, K, sent, 0)
    for copy in outs + [last]:
        copy.wait()


def handout(*refs):
    for source, target in zip(refs[:4], refs[4:]):
        target[...] = source[...]


def split(width):
    unit = 256
    return max(unit, (width * 3 // 8) // unit * unit)


def body(Z_AXIS, layer_input, output_grad, expert_ids, w_gate, w_up, w_down):
    Y, Z = Z_AXIS
    _, tokens, D = layer_input.shape
    hidden = w_gate.shape[2]
    CA = split(D)
    K = Z // 2
    rows = Y * Z * SLOT
    CB, CW = D - CA, D // CUTS
    V, DMA = pltpu.VMEM, pltpu.SemaphoreType.DMA
    scratch = [
        V((tokens, D), BF16), V((tokens, D), BF16), V((D, 2 * hidden), BF16), V((D, hidden), BF16),
        V((tokens, D), BF16), V((1, tokens), jnp.int32),
        V((Z, Y, 2 * SLOT, CA), BF16), V((Z, Y, 2 * SLOT, CB), BF16),
        V((rows, D), BF16), V((rows, D), BF16), V((rows, 2 * hidden), BF16), V((rows, hidden), BF16),
        V((Z, RING, Y * SLOT, CW), F32), V((Z, Y, 2 * SLOT, CW // 2), F32),
        *[V((K, RING, Y * SLOT, CW), BF16)] * 4,
        *[V((Y, RING, 2 * SLOT, CW // 2), BF16)] * 2,
        *[V((QUARTERS, Y - 1, Z // QUARTERS, 2 * SLOT, CW // 2), BF16)] * 2,
        *[V((K, 2 * SLOT, CW // 2), BF16)] * 4,
        *[V((2 * SLOT, CW // 2), BF16)] * 2,
        V((tokens, D), BF16), V((D, hidden), BF16), V((D, hidden), BF16), V((D, hidden), BF16),
        DMA((5,)), DMA((2,)), DMA((2,)), DMA((3,)), DMA((3,)),
        *[DMA((K, Y))] * 4, *[DMA((K,))] * 4, DMA((3, Z)), DMA((3, Z)),
        *[DMA((K, RING))] * 4, DMA((Y,)), DMA((Y,)),
        *[DMA((QUARTERS, Y - 1))] * 2, *[DMA((K,))] * 4, DMA((1,)), DMA((1,)),
    ]
    anywhere = pl.BlockSpec(memory_space=pl.ANY)
    weight = jax.ShapeDtypeStruct((D, hidden), BF16)
    token_grad, grad_gate, grad_up, grad_down = pl.pallas_call(
        functools.partial(kernel, (Y, Z, D, CA)),
        out_shape=(jax.ShapeDtypeStruct((tokens, D), BF16), weight, weight, weight),
        in_specs=[pl.BlockSpec(memory_space=pltpu.VMEM)] + [anywhere] * 5,
        out_specs=(anywhere,) * 4,
        scratch_shapes=scratch,
        compiler_params=pltpu.CompilerParams(collective_id=0, has_side_effects=True, vmem_limit_bytes=56 << 20),
    )(expert_ids, layer_input[0], output_grad[0], w_gate[0], w_up[0], w_down[0])
    steps = 4
    blocks = [pl.BlockSpec((n // steps, m), lambda i: (i, 0)) for n, m in ((tokens, D),) + ((D, hidden),) * 3]
    token_grad, grad_gate, grad_up, grad_down = pl.pallas_call(
        handout,
        grid=(steps,),
        out_shape=(jax.ShapeDtypeStruct((tokens, D), BF16), weight, weight, weight),
        in_specs=blocks,
        out_specs=blocks,
    )(token_grad, grad_gate, grad_up, grad_down)
    return token_grad[None], grad_gate[None], grad_up[None], grad_down[None]


def solution(mesh):
    rows = P("section", ("expert", "dp"), None)
    weights = P("section", None, ("expert", "dp"))
    in_specs = (rows, rows, P("section", ("expert", "dp")), weights, weights, weights)
    out_specs = (rows, weights, weights, weights)
    size = (mesh.shape["dp"] // Z_HI, mesh.shape["expert"] * Z_HI)
    return jax.shard_map(functools.partial(body, size), mesh=mesh, in_specs=in_specs, out_specs=out_specs, check_vma=False)
```

```python
import functools

import jax
import jax.numpy as jnp
from jax import lax
from jax.experimental import pallas as pl
from jax.experimental.pallas import tpu as pltpu
from jax.sharding import PartitionSpec as P

SLOT = 8
CUTS = 4
QUARTERS = 4
Z_HI = 2
F32 = jnp.float32
BF16 = jnp.bfloat16
ROWS_DIM = (((0,), (0,)), ((), ()))
BACK_DIM = (((1,), (1,)), ((), ()))


def slot_match(ids):
    tokens = ids.shape[1]
    chosen = jnp.broadcast_to((ids == 0).astype(F32), (SLOT, tokens))
    before = lax.broadcasted_iota(jnp.int32, (tokens, tokens), 0)
    after = lax.broadcasted_iota(jnp.int32, (tokens, tokens), 1)
    order = (before < after).astype(F32).astype(BF16)
    within = jnp.dot(chosen.astype(BF16), order, preferred_element_type=F32)
    place = lax.broadcasted_iota(jnp.int32, (SLOT, tokens), 0).astype(F32)
    return jnp.where(within == place, chosen, 0.0).astype(BF16)


def kernel(cfg, ids_ref, x_ref, dy_ref, wg_ref, wu_ref, wd_ref, og_v, gg_v, gu_v, gd_v,
           x_v, dy_v, w_gu, w_dn, shift_dy, shift_ids, g_a, g_b, x_all, dy_all, d_gu, hid, part,
           s_r, r_r, s_l, r_l, s_y, r_y,
           loc, sh_s, sh_r, a1_s, a1_r, ar_s, ar_r, al_s, al_r, br_s, br_r, bl_s, bl_r, by_s, by_r,
           rr_s, rr_r, rl_s, rl_r, ry_s, ry_r):
    Y, Z, D, CA = cfg
    CW = D // CUTS
    K = Z // 2
    n_sec, n_exp = lax.axis_size("section"), lax.axis_size("expert")
    sec, ex, dp = lax.axis_index("section"), lax.axis_index("expert"), lax.axis_index("dp")
    y, z = dp // Z_HI, lax.rem(dp, Z_HI) * n_exp + ex

    def wrap(v, n):
        return lax.rem(v + n, n)

    def at(yy, zz):
        return {"expert": lax.rem(zz, n_exp), "dp": yy * Z_HI + zz // n_exp}

    z_right, z_left = at(y, wrap(z + 1, Z)), at(y, wrap(z - 1, Z))
    y_right, y_left = at(wrap(y + 1, Y), z), at(wrap(y - 1, Y), z)
    y_far = at(wrap(y + 2, Y), z)
    s_prev, s_next = wrap(sec - 1, n_sec), wrap(sec + 1, n_sec)
    turn = (0, 1, -1, 2)
    owners = [{"section": s_prev, **at(wrap(y + t, Y), z)} for t in turn]
    givers = [{"section": s_next, **at(wrap(y - t, Y), z)} for t in turn]

    def remote(src, dst, s_sem, r_sem, to):
        return pltpu.make_async_remote_copy(
            src_ref=src, dst_ref=dst, send_sem=s_sem, recv_sem=r_sem, device_id=to, device_id_type=pl.DeviceIdType.MESH)

    barrier = pltpu.get_barrier_semaphore()
    partners = [z_right, z_left, y_right, y_left, y_far] + givers
    for to in partners:
        pl.semaphore_signal(barrier, inc=1, device_id=to, device_id_type=pl.DeviceIdType.MESH)

    half = w_gu.shape[1] // 2
    loads = [
        pltpu.make_async_copy(x_ref, x_v, loc.at[0]),
        pltpu.make_async_copy(dy_ref, dy_v, loc.at[1]),
        pltpu.make_async_copy(wg_ref, w_gu.at[:, pl.ds(0, half)], loc.at[2]),
        pltpu.make_async_copy(wu_ref, w_gu.at[:, pl.ds(half, half)], loc.at[3]),
        pltpu.make_async_copy(wd_ref, w_dn, loc.at[4]),
    ]
    for copy in loads:
        copy.start()
    match = slot_match(ids_ref[...])
    loads[0].wait()
    loads[1].wait()
    own = jnp.concatenate([
        jnp.dot(match, x_v[...], preferred_element_type=F32),
        jnp.dot(match, dy_v[...], preferred_element_type=F32)], axis=0).astype(BF16)
    g_a[z, y] = own[:, :CA]
    g_b[z, y] = own[:, CA:]
    pl.semaphore_wait(barrier, len(partners))

    def a1(j, to):
        return remote(g_a.at[z, y], g_a.at[z, y], a1_s.at[j], a1_r.at[j], to)

    def a1_in(j, yy):
        return remote(g_a.at[z, yy], g_a.at[z, yy], a1_s.at[j], a1_r.at[j], y_right)

    def a_right(k, block, j):
        ref = g_a.at[block, wrap(y + turn[j], Y)]
        return remote(ref, ref, ar_s.at[k, j], ar_r.at[k, j], z_right)

    def a_left(k, block, j):
        ref = g_a.at[block, wrap(y + turn[j], Y)]
        return remote(ref, ref, al_s.at[k, j], al_r.at[k, j], z_left)

    def b_right(k, block):
        return remote(g_b.at[block, y], g_b.at[block, y], br_s.at[k], br_r.at[k], z_right)

    def b_left(k, block):
        return remote(g_b.at[block, y], g_b.at[block, y], bl_s.at[k], bl_r.at[k], z_left)

    def b_y(kind, o, yy, to):
        block = wrap(z - o, Z)
        return remote(g_b.at[block, yy], g_b.at[block, yy], by_s.at[kind, o], by_r.at[kind, o], to)

    def spread(o):
        b_y(0, o, y, y_right).start()
        b_y(1, o, y, y_left).start()

    for j, to in enumerate((y_right, y_left, y_far)):
        a1(j, to).start()
    b_right(0, z).start()
    b_left(0, z).start()
    spread(0)
    shift = [remote(ids_ref, shift_ids, sh_s.at[0], sh_r.at[0], owners[0]), remote(dy_ref, shift_dy, sh_s.at[1], sh_r.at[1], owners[0])]
    for copy in shift:
        copy.start()
    a_right(0, z, 0).start()
    a_left(0, z, 0).start()
    for j, came in ((1, 1), (2, 0), (3, 2)):
        a1_in(came, wrap(y + turn[j], Y)).wait_recv()
        a_right(0, z, j).start()
        a_left(0, z, j).start()

    def pass_right(o):
        b_y(0, o, wrap(y - 1, Y), y_right).wait_recv()
        b_y(2, o, wrap(y - 1, Y), y_right).start()

    def pass_left(o):
        b_y(1, o, wrap(y + 1, Y), y_left).wait_recv()
        b_y(2, o, wrap(y + 1, Y), y_left).start()

    CZ = Z // QUARTERS
    QR = CZ * Y * SLOT

    def quarter(i):
        rows = pl.ds(pl.multiple_of(i * QR, QR), QR)

        def unpack(n, _):
            place = i * CZ + n
            away = lax.rem(place, 2) * (place + 1) // 2 - (1 - lax.rem(place, 2)) * (place // 2)
            block = wrap(z + away, Z)
            o = wrap(-away, Z)

            @pl.when(o < K)
            def _():
                b_y(1, o, wrap(y + 1, Y), y_left).wait_recv()

            @pl.when(o >= K)
            def _():
                b_y(0, o, wrap(y - 1, Y), y_right).wait_recv()

            b_y(2, o, wrap(y + 2, Y), y_right).wait_recv()
            here = pl.ds(pl.multiple_of(place * (Y * SLOT), Y * SLOT), Y * SLOT)
            for ref, lo, hi in ((g_a, 0, CA), (g_b, CA, D)):
                both = ref[block].astype(F32)
                x_all[here, lo:hi] = both[:, :SLOT].reshape(Y * SLOT, hi - lo).astype(BF16)
                dy_all[here, lo:hi] = both[:, SLOT:].reshape(Y * SLOT, hi - lo).astype(BF16)
            return 0

        lax.fori_loop(0, CZ, unpack, 0)
        both = jnp.dot(x_all[rows, :], w_gu[...], preferred_element_type=F32)
        d_hidden = jnp.dot(dy_all[rows, :], w_dn[...], preferred_element_type=F32)
        gate, upper = both[:, :half], both[:, half:]
        sigma = jax.nn.sigmoid(gate)
        active = gate * sigma
        hid[rows, :] = (active * upper).astype(BF16)
        d_gu[rows, :half] = (d_hidden * upper * sigma * (1.0 + gate * (1.0 - sigma))).astype(BF16)
        d_gu[rows, half:] = (d_hidden * active).astype(BF16)
        for cut in range(CUTS):
            piece = lax.dot_general(
                d_gu[rows, :], w_gu[cut * CW:(cut + 1) * CW, :], BACK_DIM, preferred_element_type=F32)
            part[pl.ds(i * CZ, CZ), cut] = piece.reshape(CZ, Y * SLOT, CW)

    def gather_step(k, _):
        zr, zl = wrap(z - k, Z), wrap(z + k, Z)

        @pl.when(k < K)
        def _():
            b_right(k - 1, zr).wait_recv()

            @pl.when(k < K - 1)
            def _():
                b_right(k, zr).start()

            spread(k)

        b_left(k - 1, zl).wait_recv()

        @pl.when(k < K)
        def _():
            b_left(k, zl).start()

        spread(Z - k)
        for j in range(Y):
            def right(j=j):
                a_right(k - 1, zr, j).wait_recv()

                @pl.when(k < (K if j < Y // 2 else K - 1))
                def _():
                    a_right(k, zr, j).start()

            def left(j=j):
                a_left(k - 1, zl, j).wait_recv()

                @pl.when(k < (K - 1 if j < Y // 2 else K))
                def _():
                    a_left(k, zl, j).start()

            if j < Y // 2:
                right()
                pl.when(k < K)(left)
            else:
                pl.when(k < K)(right)
                left()

        pass_right(k - 1)

        @pl.when(k > 1)
        def _():
            pass_left(Z - k + 1)

        early = K // 2 + 1

        if K == 2 * QUARTERS:
            @pl.when((k >= early) & (lax.rem(k - early, 2) == 0) & (k < K))
            def _():
                quarter((k - early) // 2)

        return 0

    for copy in loads[2:]:
        copy.wait()
    lax.fori_loop(1, K + 1, gather_step, 0)
    pass_left(K)
    if K != 2 * QUARTERS:
        for i in range(QUARTERS - 1):
            quarter(i)

    quarter(QUARTERS - 1)

    def to_right(k, cut):
        return remote(s_r.at[k, cut], r_r.at[k, cut], rr_s.at[k, cut], rr_r.at[k, cut], z_right)

    def to_left(k, cut):
        return remote(s_l.at[k, cut], r_l.at[k, cut], rl_s.at[k, cut], rl_r.at[k, cut], z_left)

    def add_right(k, cut, got):
        value = part[2 * (K - k) - 1, cut]
        if got:
            to_right(k - 1, cut).wait_recv()
            value = value + r_r[k - 1, cut].astype(F32)
        s_r[k, cut] = value.astype(BF16)
        to_right(k, cut).start()

    def add_left(k, cut, got):
        value = part[2 * (K - k) - (1 if isinstance(k, int) and k == 0 else 0), cut]
        if got:
            to_left(k - 1, cut).wait_recv()
            value = value + r_l[k - 1, cut].astype(F32)
        s_l[k, cut] = value.astype(BF16)
        to_left(k, cut).start()

    WD = D // K

    def weights(j):
        cols = pl.ds(pl.multiple_of(j * WD, WD), WD)
        both = lax.dot_general(x_all[:, cols], d_gu[...], ROWS_DIM, preferred_element_type=F32).astype(BF16)
        gg_v[cols, :] = both[:, :half]
        gu_v[cols, :] = both[:, half:]
        gd_v[cols, :] = lax.dot_general(dy_all[:, cols], hid[...], ROWS_DIM, preferred_element_type=F32).astype(BF16)

    first, second = range(CUTS // 2), range(CUTS // 2, CUTS)
    for cut in first:
        add_right(0, cut, False)
    for cut in second:
        add_left(0, cut, False)
    for cut in second:
        add_right(1, cut, False)
    for cut in first:
        add_left(1, cut, False)
    if K == 2 * QUARTERS:
        quarter(QUARTERS - 2)
    for a, b in zip(first, second):
        add_right(1, a, True)
        add_left(1, b, True)
    weights(0)
    weights(1)

    def reduce_step(k, _):
        for a, b in zip(list(second) + list(first), list(first) + list(second)):
            add_right(k, a, True)
            add_left(k, b, True)
        weights(k)
        return 0

    lax.fori_loop(2, K, reduce_step, 0)
    def to_owner(j):
        yy = wrap(y + turn[j], Y)
        return remote(s_y.at[yy], r_y.at[j], ry_s.at[j], ry_r.at[j], owners[j])

    for a, b in zip(list(second) + list(first), list(first) + list(second)):
        to_right(K - 1, a).wait_recv()
        to_left(K - 1, b).wait_recv()
    for cut in range(CUTS):
        total = part[0, cut] + r_r[K - 1, cut].astype(F32) + r_l[K - 1, cut].astype(F32)
        total = total.reshape(Y, SLOT, CW)
        total = jnp.concatenate([total[:, :, :CW // 2], total[:, :, CW // 2:]], axis=1).astype(BF16)
        s_y[:, cut] = total
    for j in (3, 1, 2, 0):
        to_owner(j).start()
    for copy in shift:
        copy.wait_recv()
    match = slot_match(shift_ids[...])
    for j in range(Y):
        to_owner(j).wait_recv()
    for cut in range(CUTS):
        rows = r_y[0, cut].astype(F32)
        for j in range(1, Y):
            rows = rows + r_y[j, cut].astype(F32)
        rows = jnp.concatenate([rows[:SLOT], rows[SLOT:]], axis=1).astype(BF16)
        term = lax.dot_general(match, rows, ROWS_DIM, preferred_element_type=F32)
        cols = slice(cut * CW, (cut + 1) * CW)
        og_v[:, cols] = (shift_dy[:, cols].astype(F32) + term).astype(BF16)

    for copy in shift:
        copy.wait_send()
    for j, to in enumerate((y_right, y_left, y_far)):
        a1(j, to).wait_send()
    for j in range(Y):
        to_owner(j).wait_send()

    def sent(k, _):
        for j in range(Y):
            pl.when(k < (K if j < Y // 2 else K - 1))(lambda j=j: a_right(k, z, j).wait_send())
            pl.when(k < (K - 1 if j < Y // 2 else K))(lambda j=j: a_left(k, z, j).wait_send())
        b_left(k, z).wait_send()
        pl.when(k < K - 1)(lambda: b_right(k, z).wait_send())
        for cut in range(CUTS):
            if cut in first:
                to_right(k, cut).wait_send()
                pl.when(k > 0)(lambda cut=cut: to_left(k, cut).wait_send())
            else:
                to_left(k, cut).wait_send()
                pl.when(k > 0)(lambda cut=cut: to_right(k, cut).wait_send())
        for kind in range(3):
            b_y(kind, k, y, y_right).wait_send()
            b_y(kind, K + k, y, y_right).wait_send()
        return 0

    lax.fori_loop(0, K, sent, 0)


def handout(*refs):
    sems = refs[-1]
    copies = [pltpu.make_async_copy(refs[i], refs[4 + i], sems.at[i]) for i in range(4)]
    for copy in copies:
        copy.start()
    for copy in copies:
        copy.wait()


def split(width):
    unit = 256
    return max(unit, (width * 3 // 8) // unit * unit)


def body(Z_AXIS, layer_input, output_grad, expert_ids, w_gate, w_up, w_down):
    Y, Z = Z_AXIS
    _, tokens, D = layer_input.shape
    hidden = w_gate.shape[2]
    CA = split(D)
    K = Z // 2
    rows = Y * Z * SLOT
    CB, CW = D - CA, D // CUTS
    V, DMA = pltpu.VMEM, pltpu.SemaphoreType.DMA
    scratch = [
        V((tokens, D), BF16), V((tokens, D), BF16), V((D, 2 * hidden), BF16), V((D, hidden), BF16),
        V((tokens, D), BF16), V((1, tokens), jnp.int32),
        V((Z, Y, 2 * SLOT, CA), BF16), V((Z, Y, 2 * SLOT, CB), BF16),
        V((rows, D), BF16), V((rows, D), BF16), V((rows, 2 * hidden), BF16), V((rows, hidden), BF16),
        V((Z, CUTS, Y * SLOT, CW), F32),
        *[V((K, CUTS, Y * SLOT, CW), BF16)] * 4,
        *[V((Y, CUTS, 2 * SLOT, CW // 2), BF16)] * 2,
        DMA((5,)), DMA((2,)), DMA((2,)), DMA((3,)), DMA((3,)),
        *[DMA((K, Y))] * 4, *[DMA((K,))] * 4, DMA((3, Z)), DMA((3, Z)),
        *[DMA((K, CUTS))] * 4, DMA((Y,)), DMA((Y,)),
    ]
    anywhere = pl.BlockSpec(memory_space=pl.ANY)
    shapes = ((tokens, D), (D, hidden), (D, hidden), (D, hidden))
    inside = pl.BlockSpec(memory_space=pltpu.VMEM)
    made = pl.pallas_call(
        functools.partial(kernel, (Y, Z, D, CA)),
        out_shape=tuple(V(shape, BF16) for shape in shapes),
        in_specs=[inside] + [anywhere] * 5,
        out_specs=(inside,) * 4,
        scratch_shapes=scratch,
        compiler_params=pltpu.CompilerParams(collective_id=0, has_side_effects=True, vmem_limit_bytes=59 << 20),
    )(expert_ids, layer_input[0], output_grad[0], w_gate[0], w_up[0], w_down[0])
    token_grad, grad_gate, grad_up, grad_down = pl.pallas_call(
        handout,
        out_shape=tuple(jax.ShapeDtypeStruct(shape, BF16) for shape in shapes),
        in_specs=[inside] * 4,
        out_specs=(anywhere,) * 4,
        scratch_shapes=[DMA((4,))],
        compiler_params=pltpu.CompilerParams(vmem_limit_bytes=8 << 20),
    )(*made)
    return token_grad[None], grad_gate[None], grad_up[None], grad_down[None]


def solution(mesh):
    rows = P("section", ("expert", "dp"), None)
    weights = P("section", None, ("expert", "dp"))
    in_specs = (rows, rows, P("section", ("expert", "dp")), weights, weights, weights)
    out_specs = (rows, weights, weights, weights)
    size = (mesh.shape["dp"] // Z_HI, mesh.shape["expert"] * Z_HI)
    return jax.shard_map(functools.partial(body, size), mesh=mesh, in_specs=in_specs, out_specs=out_specs, check_vma=False)
```

```python
import functools

import jax
import jax.numpy as jnp
from jax import lax
from jax.experimental import pallas as pl
from jax.experimental.pallas import tpu as pltpu
from jax.sharding import PartitionSpec as P

SLOT = 8
CUTS = 4
QUARTERS = 4
Z_HI = 2
F32 = jnp.float32
BF16 = jnp.bfloat16
ROWS_DIM = (((0,), (0,)), ((), ()))
BACK_DIM = (((1,), (1,)), ((), ()))


def slot_match(ids):
    tokens = ids.shape[1]
    chosen = jnp.broadcast_to((ids == 0).astype(F32), (SLOT, tokens))
    before = lax.broadcasted_iota(jnp.int32, (tokens, tokens), 0)
    after = lax.broadcasted_iota(jnp.int32, (tokens, tokens), 1)
    order = (before < after).astype(F32).astype(BF16)
    within = jnp.dot(chosen.astype(BF16), order, preferred_element_type=F32)
    place = lax.broadcasted_iota(jnp.int32, (SLOT, tokens), 0).astype(F32)
    return jnp.where(within == place, chosen, 0.0).astype(BF16)


def kernel(cfg, ids_ref, x_ref, dy_ref, wg_ref, wu_ref, wd_ref, og_v, gg_v, gu_v, gd_v,
           x_v, dy_v, w_gu, w_dn, shift_dy, shift_ids, g_a, g_b, x_all, dy_all, d_gu, hid, part,
           s_r, r_r, s_l, r_l, s_y, r_y,
           loc, sh_s, sh_r, a1_s, a1_r, ar_s, ar_r, al_s, al_r, br_s, br_r, bl_s, bl_r, by_s, by_r,
           rr_s, rr_r, rl_s, rl_r, ry_s, ry_r):
    Y, Z, D, CA = cfg
    CW = D // CUTS
    K = Z // 2
    n_sec, n_exp = lax.axis_size("section"), lax.axis_size("expert")
    sec, ex, dp = lax.axis_index("section"), lax.axis_index("expert"), lax.axis_index("dp")
    y, z = dp // Z_HI, lax.rem(dp, Z_HI) * n_exp + ex

    def wrap(v, n):
        return lax.rem(v + n, n)

    def at(yy, zz):
        return {"expert": lax.rem(zz, n_exp), "dp": yy * Z_HI + zz // n_exp}

    z_right, z_left = at(y, wrap(z + 1, Z)), at(y, wrap(z - 1, Z))
    y_right, y_left = at(wrap(y + 1, Y), z), at(wrap(y - 1, Y), z)
    y_far = at(wrap(y + 2, Y), z)
    s_prev, s_next = wrap(sec - 1, n_sec), wrap(sec + 1, n_sec)
    turn = (0, 1, -1, 2)
    owners = [{"section": s_prev, **at(wrap(y + t, Y), z)} for t in turn]
    givers = [{"section": s_next, **at(wrap(y - t, Y), z)} for t in turn]

    def remote(src, dst, s_sem, r_sem, to):
        return pltpu.make_async_remote_copy(
            src_ref=src, dst_ref=dst, send_sem=s_sem, recv_sem=r_sem, device_id=to, device_id_type=pl.DeviceIdType.MESH)

    barrier = pltpu.get_barrier_semaphore()
    partners = [z_right, z_left, y_right, y_left, y_far] + givers
    for to in partners:
        pl.semaphore_signal(barrier, inc=1, device_id=to, device_id_type=pl.DeviceIdType.MESH)

    half = w_gu.shape[1] // 2
    loads = [
        pltpu.make_async_copy(x_ref, x_v, loc.at[0]),
        pltpu.make_async_copy(dy_ref, dy_v, loc.at[1]),
        pltpu.make_async_copy(wg_ref, w_gu.at[:, pl.ds(0, half)], loc.at[2]),
        pltpu.make_async_copy(wu_ref, w_gu.at[:, pl.ds(half, half)], loc.at[3]),
        pltpu.make_async_copy(wd_ref, w_dn, loc.at[4]),
    ]
    for copy in loads:
        copy.start()
    match = slot_match(ids_ref[...])
    loads[0].wait()
    loads[1].wait()
    own = jnp.concatenate([
        jnp.dot(match, x_v[...], preferred_element_type=F32),
        jnp.dot(match, dy_v[...], preferred_element_type=F32)], axis=0).astype(BF16)
    g_a[z, y] = own[:, :CA]
    g_b[z, y] = own[:, CA:]
    pl.semaphore_wait(barrier, len(partners))

    def a1(j, to):
        return remote(g_a.at[z, y], g_a.at[z, y], a1_s.at[j], a1_r.at[j], to)

    def a1_in(j, yy):
        return remote(g_a.at[z, yy], g_a.at[z, yy], a1_s.at[j], a1_r.at[j], y_right)

    def a_right(k, block, j):
        ref = g_a.at[block, wrap(y + turn[j], Y)]
        return remote(ref, ref, ar_s.at[k, j], ar_r.at[k, j], z_right)

    def a_left(k, block, j):
        ref = g_a.at[block, wrap(y + turn[j], Y)]
        return remote(ref, ref, al_s.at[k, j], al_r.at[k, j], z_left)

    def b_right(k, block):
        return remote(g_b.at[block, y], g_b.at[block, y], br_s.at[k], br_r.at[k], z_right)

    def b_left(k, block):
        return remote(g_b.at[block, y], g_b.at[block, y], bl_s.at[k], bl_r.at[k], z_left)

    def b_y(kind, o, yy, to):
        block = wrap(z - o, Z)
        return remote(g_b.at[block, yy], g_b.at[block, yy], by_s.at[kind, o], by_r.at[kind, o], to)

    def spread(o):
        b_y(0, o, y, y_right).start()
        b_y(1, o, y, y_left).start()

    for j, to in enumerate((y_right, y_left, y_far)):
        a1(j, to).start()
    b_right(0, z).start()
    b_left(0, z).start()
    spread(0)
    shift = [remote(ids_ref, shift_ids, sh_s.at[0], sh_r.at[0], owners[0]), remote(dy_ref, shift_dy, sh_s.at[1], sh_r.at[1], owners[0])]
    for copy in shift:
        copy.start()
    a_right(0, z, 0).start()
    a_left(0, z, 0).start()
    for j, came in ((1, 1), (2, 0), (3, 2)):
        a1_in(came, wrap(y + turn[j], Y)).wait_recv()
        a_right(0, z, j).start()
        a_left(0, z, j).start()

    def pass_right(o):
        b_y(0, o, wrap(y - 1, Y), y_right).wait_recv()
        b_y(2, o, wrap(y - 1, Y), y_right).start()

    def pass_left(o):
        b_y(1, o, wrap(y + 1, Y), y_left).wait_recv()
        b_y(2, o, wrap(y + 1, Y), y_left).start()

    CZ = Z // QUARTERS
    QR = CZ * Y * SLOT

    def quarter(i):
        rows = pl.ds(pl.multiple_of(i * QR, QR), QR)

        def unpack(n, _):
            place = i * CZ + n
            away = lax.rem(place, 2) * (place + 1) // 2 - (1 - lax.rem(place, 2)) * (place // 2)
            block = wrap(z + away, Z)
            o = wrap(-away, Z)

            @pl.when(o < K)
            def _():
                b_y(1, o, wrap(y + 1, Y), y_left).wait_recv()

            @pl.when(o >= K)
            def _():
                b_y(0, o, wrap(y - 1, Y), y_right).wait_recv()

            b_y(2, o, wrap(y + 2, Y), y_right).wait_recv()
            here = pl.ds(pl.multiple_of(place * (Y * SLOT), Y * SLOT), Y * SLOT)
            for ref, lo, hi in ((g_a, 0, CA), (g_b, CA, D)):
                both = ref[block].astype(F32)
                x_all[here, lo:hi] = both[:, :SLOT].reshape(Y * SLOT, hi - lo).astype(BF16)
                dy_all[here, lo:hi] = both[:, SLOT:].reshape(Y * SLOT, hi - lo).astype(BF16)
            return 0

        lax.fori_loop(0, CZ, unpack, 0)
        both = jnp.dot(x_all[rows, :], w_gu[...], preferred_element_type=F32)
        d_hidden = jnp.dot(dy_all[rows, :], w_dn[...], preferred_element_type=F32)
        gate, upper = both[:, :half], both[:, half:]
        sigma = jax.nn.sigmoid(gate)
        active = gate * sigma
        hid[rows, :] = (active * upper).astype(BF16)
        d_gu[rows, :half] = (d_hidden * upper * sigma * (1.0 + gate * (1.0 - sigma))).astype(BF16)
        d_gu[rows, half:] = (d_hidden * active).astype(BF16)
        for cut in range(CUTS):
            piece = lax.dot_general(
                d_gu[rows, :], w_gu[cut * CW:(cut + 1) * CW, :], BACK_DIM, preferred_element_type=F32)
            part[pl.ds(i * CZ, CZ), cut] = piece.reshape(CZ, Y * SLOT, CW)

    def gather_step(k, _):
        zr, zl = wrap(z - k, Z), wrap(z + k, Z)

        @pl.when(k < K)
        def _():
            b_right(k - 1, zr).wait_recv()

            @pl.when(k < K - 1)
            def _():
                b_right(k, zr).start()

            spread(k)

        b_left(k - 1, zl).wait_recv()

        @pl.when(k < K)
        def _():
            b_left(k, zl).start()

        spread(Z - k)
        for j in range(Y):
            def right(j=j):
                a_right(k - 1, zr, j).wait_recv()

                @pl.when(k < (K if j < Y // 2 else K - 1))
                def _():
                    a_right(k, zr, j).start()

            def left(j=j):
                a_left(k - 1, zl, j).wait_recv()

                @pl.when(k < (K - 1 if j < Y // 2 else K))
                def _():
                    a_left(k, zl, j).start()

            if j < Y // 2:
                right()
                pl.when(k < K)(left)
            else:
                pl.when(k < K)(right)
                left()

        pass_right(k - 1)

        @pl.when(k > 1)
        def _():
            pass_left(Z - k + 1)

        early = K // 2 + 1

        if K == 2 * QUARTERS:
            @pl.when((k >= early) & (lax.rem(k - early, 2) == 0) & (k < K))
            def _():
                quarter((k - early) // 2)

        return 0

    for copy in loads[2:]:
        copy.wait()
    lax.fori_loop(1, K + 1, gather_step, 0)
    pass_left(K)
    if K != 2 * QUARTERS:
        for i in range(QUARTERS - 1):
            quarter(i)

    quarter(QUARTERS - 1)

    def to_right(k, cut):
        return remote(s_r.at[k, cut], r_r.at[k, cut], rr_s.at[k, cut], rr_r.at[k, cut], z_right)

    def to_left(k, cut):
        return remote(s_l.at[k, cut], r_l.at[k, cut], rl_s.at[k, cut], rl_r.at[k, cut], z_left)

    def add_right(k, cut, got):
        value = part[2 * (K - k) - 1, cut]
        if got:
            to_right(k - 1, cut).wait_recv()
            value = value + r_r[k - 1, cut].astype(F32)
        s_r[k, cut] = value.astype(BF16)
        to_right(k, cut).start()

    def add_left(k, cut, got):
        value = part[2 * (K - k) - (1 if isinstance(k, int) and k == 0 else 0), cut]
        if got:
            to_left(k - 1, cut).wait_recv()
            value = value + r_l[k - 1, cut].astype(F32)
        s_l[k, cut] = value.astype(BF16)
        to_left(k, cut).start()

    WD = D // K

    def weights(j):
        cols = pl.ds(pl.multiple_of(j * WD, WD), WD)
        both = lax.dot_general(x_all[:, cols], d_gu[...], ROWS_DIM, preferred_element_type=F32).astype(BF16)
        gg_v[cols, :] = both[:, :half]
        gu_v[cols, :] = both[:, half:]
        gd_v[cols, :] = lax.dot_general(dy_all[:, cols], hid[...], ROWS_DIM, preferred_element_type=F32).astype(BF16)

    first, second = range(CUTS // 2), range(CUTS // 2, CUTS)
    for cut in first:
        add_right(0, cut, False)
    for cut in second:
        add_left(0, cut, False)
    for cut in second:
        add_right(1, cut, False)
    for cut in first:
        add_left(1, cut, False)
    if K == 2 * QUARTERS:
        quarter(QUARTERS - 2)
    for a, b in zip(first, second):
        add_right(1, a, True)
        add_left(1, b, True)
    weights(0)
    weights(1)

    def reduce_step(k, _):
        for a, b in zip(list(second) + list(first), list(first) + list(second)):
            add_right(k, a, True)
            add_left(k, b, True)
        weights(k)
        return 0

    lax.fori_loop(2, K, reduce_step, 0)
    def to_owner(group, j):
        cuts = pl.ds(group * (CUTS // 2), CUTS // 2)
        yy = wrap(y + turn[j], Y)
        return remote(s_y.at[yy, cuts], r_y.at[j, cuts], ry_s.at[group, j], ry_r.at[group, j], owners[j])

    for copy in shift:
        copy.wait_recv()
    match = slot_match(shift_ids[...])
    for cut in list(second) + list(first):
        to_right(K - 1, cut).wait_recv()
        to_left(K - 1, cut).wait_recv()
        total = part[0, cut] + r_r[K - 1, cut].astype(F32) + r_l[K - 1, cut].astype(F32)
        total = total.reshape(Y, SLOT, CW)
        total = jnp.concatenate([total[:, :, :CW // 2], total[:, :, CW // 2:]], axis=1).astype(BF16)
        s_y[:, cut] = total
        if cut in (second[-1], first[-1]):
            for j in (3, 1, 2, 0):
                to_owner(1 if cut in second else 0, j).start()
    for cut in list(second) + list(first):
        if cut in (second[0], first[0]):
            for j in range(Y):
                to_owner(1 if cut in second else 0, j).wait_recv()
        rows = r_y[0, cut].astype(F32)
        for j in range(1, Y):
            rows = rows + r_y[j, cut].astype(F32)
        rows = jnp.concatenate([rows[:SLOT], rows[SLOT:]], axis=1).astype(BF16)
        term = lax.dot_general(match, rows, ROWS_DIM, preferred_element_type=F32)
        cols = slice(cut * CW, (cut + 1) * CW)
        og_v[:, cols] = (shift_dy[:, cols].astype(F32) + term).astype(BF16)

    for copy in shift:
        copy.wait_send()
    for j, to in enumerate((y_right, y_left, y_far)):
        a1(j, to).wait_send()
    for j in range(Y):
        to_owner(0, j).wait_send()
        to_owner(1, j).wait_send()

    def sent(k, _):
        for j in range(Y):
            pl.when(k < (K if j < Y // 2 else K - 1))(lambda j=j: a_right(k, z, j).wait_send())
            pl.when(k < (K - 1 if j < Y // 2 else K))(lambda j=j: a_left(k, z, j).wait_send())
        b_left(k, z).wait_send()
        pl.when(k < K - 1)(lambda: b_right(k, z).wait_send())
        for cut in range(CUTS):
            if cut in first:
                to_right(k, cut).wait_send()
                pl.when(k > 0)(lambda cut=cut: to_left(k, cut).wait_send())
            else:
                to_left(k, cut).wait_send()
                pl.when(k > 0)(lambda cut=cut: to_right(k, cut).wait_send())
        for kind in range(3):
            b_y(kind, k, y, y_right).wait_send()
            b_y(kind, K + k, y, y_right).wait_send()
        return 0

    lax.fori_loop(0, K, sent, 0)


def handout(*refs):
    sems = refs[-1]
    copies = [pltpu.make_async_copy(refs[i], refs[4 + i], sems.at[i]) for i in range(4)]
    for copy in copies:
        copy.start()
    for copy in copies:
        copy.wait()


def split(width):
    unit = 256
    return max(unit, (width * 3 // 8) // unit * unit)


def body(Z_AXIS, layer_input, output_grad, expert_ids, w_gate, w_up, w_down):
    Y, Z = Z_AXIS
    _, tokens, D = layer_input.shape
    hidden = w_gate.shape[2]
    CA = split(D)
    K = Z // 2
    rows = Y * Z * SLOT
    CB, CW = D - CA, D // CUTS
    V, DMA = pltpu.VMEM, pltpu.SemaphoreType.DMA
    scratch = [
        V((tokens, D), BF16), V((tokens, D), BF16), V((D, 2 * hidden), BF16), V((D, hidden), BF16),
        V((tokens, D), BF16), V((1, tokens), jnp.int32),
        V((Z, Y, 2 * SLOT, CA), BF16), V((Z, Y, 2 * SLOT, CB), BF16),
        V((rows, D), BF16), V((rows, D), BF16), V((rows, 2 * hidden), BF16), V((rows, hidden), BF16),
        V((Z, CUTS, Y * SLOT, CW), F32),
        *[V((K, CUTS, Y * SLOT, CW), BF16)] * 4,
        *[V((Y, CUTS, 2 * SLOT, CW // 2), BF16)] * 2,
        DMA((5,)), DMA((2,)), DMA((2,)), DMA((3,)), DMA((3,)),
        *[DMA((K, Y))] * 4, *[DMA((K,))] * 4, DMA((3, Z)), DMA((3, Z)),
        *[DMA((K, CUTS))] * 4, DMA((2, Y)), DMA((2, Y)),
    ]
    anywhere = pl.BlockSpec(memory_space=pl.ANY)
    shapes = ((tokens, D), (D, hidden), (D, hidden), (D, hidden))
    inside = pl.BlockSpec(memory_space=pltpu.VMEM)
    made = pl.pallas_call(
        functools.partial(kernel, (Y, Z, D, CA)),
        out_shape=tuple(V(shape, BF16) for shape in shapes),
        in_specs=[inside] + [anywhere] * 5,
        out_specs=(inside,) * 4,
        scratch_shapes=scratch,
        compiler_params=pltpu.CompilerParams(collective_id=0, has_side_effects=True, vmem_limit_bytes=59 << 20),
    )(expert_ids, layer_input[0], output_grad[0], w_gate[0], w_up[0], w_down[0])
    token_grad, grad_gate, grad_up, grad_down = pl.pallas_call(
        handout,
        out_shape=tuple(jax.ShapeDtypeStruct(shape, BF16) for shape in shapes),
        in_specs=[inside] * 4,
        out_specs=(anywhere,) * 4,
        scratch_shapes=[DMA((4,))],
        compiler_params=pltpu.CompilerParams(vmem_limit_bytes=8 << 20),
    )(*made)
    return token_grad[None], grad_gate[None], grad_up[None], grad_down[None]


def solution(mesh):
    rows = P("section", ("expert", "dp"), None)
    weights = P("section", None, ("expert", "dp"))
    in_specs = (rows, rows, P("section", ("expert", "dp")), weights, weights, weights)
    out_specs = (rows, weights, weights, weights)
    size = (mesh.shape["dp"] // Z_HI, mesh.shape["expert"] * Z_HI)
    return jax.shard_map(functools.partial(body, size), mesh=mesh, in_specs=in_specs, out_specs=out_specs, check_vma=False)
```
